256 devices in a mesh: comp: 2 (over core), row: 8 (over z), col: 16 (over y, x).
Axes of the slice: x: 4, y: 4, z: 8, core: 2. Of those that a mesh axis runs over, the one named last changes fastest.
Arguments:
- atmosphere_state: bfloat16 [384, 1024, 512], P('row', 'col', 'comp'), may hold values from -6 to 6
- water_condition: bfloat16 [192, 2048, 256], P('row', 'col', 'comp'), may hold values from -6 to 6
- ocean_cell_mask: int32 [192, 2048], P('row', 'col'), may hold values 0 or 1
- atmos_to_ocean_index: int32 [192, 2048, 4], P('row', 'col'), may hold values from 0 to 3299, as said below
- atmos_to_ocean_weight: float32 [192, 2048, 4], P('row', 'col'), may hold values from 0.1 to 1
- water_source_positions: int32 [384, 1024, 4], P('row', 'col'), may hold values from 0 to 3379, as said below
- water_source_overlay_areas: float32 [384, 1024, 4], P('row', 'col'), may hold values from 0.1 to 1
- flux_weight: bfloat16 [512, 16], P('comp'), may hold values from -0.25 to 0.25
- flux_lift_weight: bfloat16 [16, 256], P(None, 'comp'), may hold values from -1.5 to 1.5
- interface_projection_matrix: bfloat16 [256, 16], P('comp'), may hold values from -0.375 to 0.375
- interface_driving_matrix: bfloat16 [16, 512], P(None, 'comp'), may hold values from -1.5 to 1.5
- forward_basis: bfloat16 [1024, 384, 384], P(('row', 'col')), may hold values from -0.3125 to 0.3125
- inverse_basis: bfloat16 [1024, 384, 384], P(('row', 'col')), may hold values from -0.3125 to 0.3125
- mixing_weight: bfloat16 [512, 512], P(None, 'comp'), may hold values from -0.25 to 0.25
- degree_filter: float32 [384, 512], P(None, 'comp'), may hold values from 0.3 to 3
- first_ocean_kernel: bfloat16 [3, 3, 256, 256], P(None, None, None, 'comp'), may hold values from -0.125 to 0.125
- second_ocean_kernel: bfloat16 [3, 3, 256, 256], P(None, None, None, 'comp'), may hold values from -0.125 to 0.125
Outputs:
- atm_out: bfloat16 [384, 1024, 512], P('row', 'col', 'comp')
- ocean_out: bfloat16 [192, 2048, 256], P('row', 'col', 'comp')
The draws below stay inside these ranges and needn't reach their ends.
Inputs may be any that keep to these rules, and one draw needn't show every extreme that they name: `atmos_to_ocean_index`: for the ocean cell in row i and column j, each entry names row-major a cell of the block of (50) x (66) cells made of atmosphere block (i // 24, j // 128) and one cycle around it. `water_source_positions`: for the atmosphere cell in row t and column j, each entry names row-major a cell of the block of (26) x (130) cells made of ocean block (t // 48, j // 64) and one cycle around it.
All inputs are finite; a program needn't handle non-finite values. No bound on the sum of `ocean_cell_mask` on one device may be relied on, other than what follows from the above.
Results may differ from the reference program's by a relative error of at most 0.022.
Values may be sent and summed in bfloat16 or wider, within the bound.
A program may use at most 128 MiB of HBM per device.

```python
import math
import jax
import jax.numpy as jnp
from jax import lax

NLAT = 384
NLON = 1024
DEGREES = 384
ATMOS_CHANNELS = 512
OCEAN_CHANNELS = 256
NF = 16
SURFACE_FIELDS = 16
KSRC = 4
WATER_PATCH_YLEN = 24
PART_PARALLELS = 48
PART_MERIDIANS = 64
WATER_PATCH_XLEN = 128
ONROWS = 192
ONCOLS = 2048


def place_sources(key, centre_row, centre_col, reach, width):
    row_count = centre_row.shape[0]
    col_count = centre_col.shape[0]
    row_key, col_key = jax.random.split(key)
    row_step = jax.random.randint(row_key, (row_count, col_count, KSRC), -1, 2)
    col_step = jax.random.randint(col_key, (row_count, col_count, KSRC), -1, reach + 1)
    slot = jnp.arange(KSRC, dtype=jnp.int32)
    row_step = jnp.where(slot == 0, -1, jnp.where(slot == 1, 1, row_step))
    col_step = jnp.where(slot == 0, -1, jnp.where(slot == 1, reach, col_step))
    flat_index = (centre_row[:, None, None] + row_step) * width + centre_col[None, :, None] + col_step
    return flat_index.astype(jnp.int32)


def draw_atmos_to_ocean_index(key, part):
    key = jax.random.fold_in(key, 11)
    rows_local = jnp.arange(ONROWS, dtype=jnp.int32) % WATER_PATCH_YLEN
    cols_local = jnp.arange(ONCOLS, dtype=jnp.int32) % WATER_PATCH_XLEN
    centre_row = 1 + rows_local * (PART_PARALLELS - 1) // (WATER_PATCH_YLEN - 1)
    centre_col = 1 + cols_local // 2
    return place_sources(key, centre_row, centre_col, 1, PART_MERIDIANS + 2)


def draw_water_source_positions(key, part):
    key = jax.random.fold_in(key, 23)
    rows_local = jnp.arange(NLAT, dtype=jnp.int32) % PART_PARALLELS
    cols_local = jnp.arange(NLON, dtype=jnp.int32) % PART_MERIDIANS
    centre_row = 1 + rows_local * (WATER_PATCH_YLEN - 1) // (PART_PARALLELS - 1)
    centre_col = 1 + 2 * cols_local
    return place_sources(key, centre_row, centre_col, 2, WATER_PATCH_XLEN + 2)


def place_ends(result, stream_key, smallest, high):
    extent = result.shape
    index_at = [jax.random.randint(jax.random.fold_in(stream_key, axis), (), 0, extent[axis]) for axis in range(len(extent))]
    result = result.at[tuple(index_at)].set(smallest)
    longest = extent.index(max(extent))
    index_at[longest] = (index_at[longest] + 1) % extent[longest]
    return result.at[tuple(index_at)].set(high)


def level_of(stream_key, dims, shards, least, high):
    def one(axis_at, shards_of):
        steps = jax.random.uniform(jax.random.fold_in(jax.random.fold_in(stream_key, 6), axis_at), (shards_of,), jnp.float32, least / len(shards), high / len(shards))
        return jnp.repeat(jnp.exp(steps), dims[axis_at] // shards_of).reshape((-1,) + (1,) * (len(dims) - axis_at - 1))

    level = one(*shards[0])
    for cut in shards[1:]:
        level = level * one(*cut)
    return level


def gaussian(rng, extent, deviation, most, cuts=(), held_as=jnp.bfloat16):
    gain = level_of(rng, extent, cuts, -0.22, 0.18) if cuts else 1.0
    result = jax.random.normal(rng, extent, jnp.float32) * deviation * gain
    return jnp.minimum(jnp.maximum(result, -most), most).astype(held_as)


def setup_inputs(seed: int = 0) -> dict:
    key_list = jax.random.split(jax.random.key(seed), 18)
    atmosphere_state = gaussian(key_list[0], (NLAT, NLON, ATMOS_CHANNELS), 1.0, 6.0, ((0, 8), (1, 16), (2, 2)))
    water_condition = gaussian(key_list[1], (ONROWS, ONCOLS, OCEAN_CHANNELS), 1.0, 6.0, ((0, 8), (1, 16), (2, 2)))
    ocean_cell_mask = place_ends((jax.random.randint(key_list[2], (ONROWS, ONCOLS), 0, 10) < 7).astype(jnp.int32), jax.random.fold_in(key_list[2], 1), 0, 1)
    atmos_to_ocean_index = draw_atmos_to_ocean_index(jax.random.fold_in(key_list[17], 71), 0)
    atmos_to_ocean_weight = jnp.clip(jnp.exp(math.log(1.0) - 2.3025851 * jax.random.uniform(key_list[4], (ONROWS, ONCOLS, KSRC), jnp.float32) ** level_of(key_list[4], (ONROWS, ONCOLS, KSRC), ((0, 8), (1, 16)), -0.2, 0.2)), 0.1, 1.0)
    water_source_positions = draw_water_source_positions(jax.random.fold_in(key_list[17], 71), 0)
    water_source_overlay_areas = jnp.clip(jnp.exp(math.log(1.0) - 2.3025851 * jax.random.uniform(key_list[6], (NLAT, NLON, KSRC), jnp.float32) ** level_of(key_list[6], (NLAT, NLON, KSRC), ((0, 8), (1, 16)), -0.2, 0.2)), 0.1, 1.0)
    flux_weight = gaussian(key_list[7], (ATMOS_CHANNELS, NF), ATMOS_CHANNELS ** -0.5, 0.25, ((0, 2),))
    flux_lift_weight = gaussian(key_list[8], (NF, OCEAN_CHANNELS), NF ** -0.5, 1.5, ((1, 2),))
    interface_projection_matrix = gaussian(key_list[9], (OCEAN_CHANNELS, SURFACE_FIELDS), OCEAN_CHANNELS ** -0.5, 0.375, ((0, 2),))
    interface_driving_matrix = gaussian(key_list[10], (SURFACE_FIELDS, ATMOS_CHANNELS), SURFACE_FIELDS ** -0.5, 1.5, ((1, 2),))
    forward_basis = gaussian(key_list[11], (NLON, DEGREES, NLAT), NLAT ** -0.5, 0.3125, ((0, 128),))
    inverse_basis = gaussian(key_list[12], (NLON, NLAT, DEGREES), DEGREES ** -0.5, 0.3125, ((0, 128),))
    mixing_weight = gaussian(key_list[13], (ATMOS_CHANNELS, ATMOS_CHANNELS), ATMOS_CHANNELS ** -0.5, 0.25, ((1, 2),))
    degree_filter = jnp.clip(jnp.exp(math.log(3.0) - 2.3025851 * jax.random.uniform(key_list[14], (DEGREES, ATMOS_CHANNELS), jnp.float32) ** level_of(key_list[14], (DEGREES, ATMOS_CHANNELS), ((1, 2),), -0.2, 0.2)), 0.3, 3.0)
    first_ocean_kernel = gaussian(key_list[15], (3, 3, OCEAN_CHANNELS, OCEAN_CHANNELS), (9 * OCEAN_CHANNELS) ** -0.5, 0.125, ((3, 2),))
    second_ocean_kernel = gaussian(key_list[16], (3, 3, OCEAN_CHANNELS, OCEAN_CHANNELS), (9 * OCEAN_CHANNELS) ** -0.5, 0.125, ((3, 2),))
    return {"atmosphere_state": atmosphere_state, "water_condition": water_condition, "ocean_cell_mask": ocean_cell_mask, "atmos_to_ocean_index": atmos_to_ocean_index, "atmos_to_ocean_weight": atmos_to_ocean_weight, "water_source_positions": water_source_positions, "water_source_overlay_areas": water_source_overlay_areas, "flux_weight": flux_weight, "flux_lift_weight": flux_lift_weight, "interface_projection_matrix": interface_projection_matrix, "interface_driving_matrix": interface_driving_matrix, "forward_basis": forward_basis, "inverse_basis": inverse_basis, "mixing_weight": mixing_weight, "degree_filter": degree_filter, "first_ocean_kernel": first_ocean_kernel, "second_ocean_kernel": second_ocean_kernel}


def lon_table(count):
    col_idx = jnp.arange(count, dtype=jnp.int32)[:, None]
    coef_idx = jnp.arange(count, dtype=jnp.int32)[None, :]
    half_count = count // 2
    freq = jnp.where(coef_idx <= half_count, coef_idx, coef_idx - half_count)
    phase = (col_idx * freq % count).astype(jnp.float32) * (2.0 * math.pi / count)
    values = jnp.where(coef_idx <= half_count, jnp.cos(phase), jnp.sin(phase))
    return (values * math.sqrt(2.0 / count)).astype(jnp.bfloat16)

def joint_advance(field, index, weight, rows_dev, cols_dev, src_rows, src_cols):
    dst_rows, dst_cols, count = index.shape
    block_row = (jnp.arange(dst_rows, dtype=jnp.int32) // rows_dev)[:, None, None]
    block_col = (jnp.arange(dst_cols, dtype=jnp.int32) // cols_dev)[None, :, None]
    local_row = index // (src_cols + 2)
    local_col = index % (src_cols + 2)
    padded = jnp.pad(field, ((1, 1), (1, 1), (0, 0)))
    values = padded[block_row * src_rows + local_row, block_col * src_cols + local_col]
    normed = weight / lax.optimization_barrier(jnp.sum(weight, axis=-1, keepdims=True))
    return lax.optimization_barrier(jnp.sum(normed[..., None] * values, axis=2))

def conv_full(state, weight):
    rows, cols = (state.shape[0], state.shape[1])
    padded = jnp.pad(state.astype(jnp.float32), ((1, 1), (1, 1), (0, 0)))
    weight32 = weight.astype(jnp.float32)
    total = jnp.zeros((rows, cols, weight.shape[3]), jnp.float32)
    for row_step in range(3):
        for col_step in range(3):
            window = padded[row_step:row_step + rows, col_step:col_step + cols]
            total = total + jnp.einsum('rcx,xy->rcy', window, weight32[row_step, col_step])
    return total

def reference(atmosphere_state, water_condition, ocean_cell_mask, atmos_to_ocean_index, atmos_to_ocean_weight, water_source_positions, water_source_overlay_areas, flux_weight, flux_lift_weight, interface_projection_matrix, interface_driving_matrix, forward_basis, inverse_basis, mixing_weight, degree_filter, first_ocean_kernel, second_ocean_kernel):
    boundary_exchange_rate = jnp.einsum('tjc,cf->tjf', atmosphere_state.astype(jnp.float32), flux_weight.astype(jnp.float32))
    water_warmth = jnp.einsum('fwe,et->fwt', water_condition.astype(jnp.float32), interface_projection_matrix.astype(jnp.float32))
    flux_ocean = joint_advance(boundary_exchange_rate, atmos_to_ocean_index, atmos_to_ocean_weight, WATER_PATCH_YLEN, WATER_PATCH_XLEN, PART_PARALLELS, PART_MERIDIANS)
    water_warmth_on_air_grid = joint_advance(water_warmth, water_source_positions, water_source_overlay_areas, PART_PARALLELS, PART_MERIDIANS, WATER_PATCH_YLEN, WATER_PATCH_XLEN)
    water_driving_term = jnp.dot(water_warmth_on_air_grid, interface_driving_matrix.astype(jnp.float32), precision=lax.Precision.HIGHEST)
    lifted = (atmosphere_state.astype(jnp.float32) + water_driving_term).astype(jnp.bfloat16)
    table = lon_table(NLON).astype(jnp.float32)
    spectra = jnp.einsum('tjc,jk->tkc', lifted.astype(jnp.float32), table).astype(jnp.bfloat16)
    modes = jnp.einsum('tkc,klt->klc', spectra.astype(jnp.float32), forward_basis.astype(jnp.float32)).astype(jnp.bfloat16)
    mixed = jnp.einsum('klc,cd->kld', modes.astype(jnp.float32), mixing_weight.astype(jnp.float32))
    mixed = (mixed * degree_filter[None]).astype(jnp.bfloat16)
    synth = jnp.einsum('kld,ktl->tkd', mixed.astype(jnp.float32), inverse_basis.astype(jnp.float32)).astype(jnp.bfloat16)
    grid = jnp.einsum('tkd,jk->tjd', synth.astype(jnp.float32), table).astype(jnp.bfloat16)
    atm_out = (lifted.astype(jnp.float32) + jax.nn.gelu(grid.astype(jnp.float32))).astype(jnp.bfloat16)
    hidden = jax.nn.gelu(conv_full(water_condition, first_ocean_kernel)).astype(jnp.bfloat16)
    inner = conv_full(hidden, second_ocean_kernel)
    lift = jnp.dot(flux_ocean, flux_lift_weight.astype(jnp.float32), precision=lax.Precision.HIGHEST)
    mask_values = ocean_cell_mask.astype(jnp.float32)[:, :, None]
    ocean_out = (water_condition.astype(jnp.float32) + mask_values * (inner + lift)).astype(jnp.bfloat16)
    return (atm_out, ocean_out)
```

```python
import math

import jax
import jax.numpy as jnp
import ml_dtypes
import numpy as np
from jax import lax
from jax.sharding import PartitionSpec as P

NLON = 1024


def padded_2(cells, sides, width):
    for axis, dim in sides:
        count = lax.axis_size(axis)
        ends = count - 1
        head = lax.slice_in_dim(cells, 0, width, axis=dim)
        tail = lax.slice_in_dim(cells, cells.shape[dim] - width, cells.shape[dim], axis=dim)
        cells = jnp.concatenate(
            [
                lax.ppermute(tail, axis, [(i, (i + 1) % count) for i in range(ends)]),
                cells,
                lax.ppermute(head, axis, [((i + 1) % count, i) for i in range(ends)]),
            ],
            axis=dim,
        )
    return cells


def lon_table(count):
    col_idx = np.arange(count, dtype=np.int64)[:, None]
    coef_idx = np.arange(count, dtype=np.int64)[None, :]
    half_count = count // 2
    freq = np.where(coef_idx <= half_count, coef_idx, coef_idx - half_count)
    phase = (col_idx * freq % count) * (2.0 * math.pi / count)
    values = np.where(coef_idx <= half_count, np.cos(phase), np.sin(phase))
    return (values * math.sqrt(2.0 / count)).astype(ml_dtypes.bfloat16)


def regrid_points(widened, index, weight):
    flat = widened.reshape(-1, widened.shape[2])
    values = flat[index]
    normed = weight / jnp.sum(weight, axis=-1, keepdims=True)
    return jnp.sum(normed[..., None] * values, axis=2)


def conv_taps(padded, weight):
    rows = padded.shape[0] - 2
    cols = padded.shape[1] - 2
    total = jnp.zeros((rows, cols, weight.shape[3]), jnp.float32)
    for row_step in range(3):
        for col_step in range(3):
            window = padded[row_step : row_step + rows, col_step : col_step + cols]
            total = total + jnp.einsum(
                "rcx,xy->rcy",
                window,
                weight[row_step, col_step],
                preferred_element_type=jnp.float32,
            )
    return total


def channels(state):
    return lax.all_gather(state, "comp", axis=2, tiled=True)


def widen(state):
    return padded_2(state, (("row", 0), ("col", 1)), 1)


def fold_mixing(mixing_weight, piece):
    return jnp.einsum("klc,cd->kld", piece, mixing_weight, preferred_element_type=jnp.float32)


def mix_direct(modes, mixing_weight):
    return fold_mixing(mixing_weight, lax.all_gather(modes, "comp", axis=2, tiled=True))


def local(
    atmosphere_state,
    water_condition,
    ocean_cell_mask,
    atmos_to_ocean_index,
    atmos_to_ocean_weight,
    water_source_positions,
    water_source_overlay_areas,
    flux_weight,
    flux_lift_weight,
    interface_projection_matrix,
    interface_driving_matrix,
    forward_basis,
    inverse_basis,
    mixing_weight,
    degree_filter,
    first_ocean_kernel,
    second_ocean_kernel,
):
    air_by_lat = lax.all_to_all(
        atmosphere_state, "col", split_axis=0, concat_axis=1, tiled=True
    )
    boundary_exchange_portion = jnp.einsum(
        "tjc,cf->tjf", atmosphere_state, flux_weight, preferred_element_type=jnp.float32
    )
    water_warmth_portion = jnp.einsum(
        "fwe,et->fwt",
        water_condition,
        interface_projection_matrix,
        preferred_element_type=jnp.float32,
    )
    boundary_exchange_rate, water_warmth = (
        lax.psum(boundary_exchange_portion.astype(jnp.bfloat16), "comp").astype(jnp.float32),
        lax.psum(water_warmth_portion.astype(jnp.bfloat16), "comp").astype(jnp.float32),
    )
    flux_wide = padded_2(
        boundary_exchange_rate.astype(jnp.bfloat16), (("row", 0), ("col", 1)), 1
    ).astype(boundary_exchange_rate.dtype)
    water_warmth_widened = padded_2(
        water_warmth.astype(jnp.bfloat16), (("row", 0), ("col", 1)), 1
    ).astype(water_warmth.dtype)
    flux_ocean = regrid_points(flux_wide, atmos_to_ocean_index, atmos_to_ocean_weight)
    water_warmth_on_air_grid = regrid_points(
        water_warmth_widened, water_source_positions, water_source_overlay_areas
    )
    water_driving_term = jnp.dot(
        water_warmth_on_air_grid,
        interface_driving_matrix.astype(jnp.float32),
        precision=lax.Precision.HIGHEST,
    )
    lifted = (atmosphere_state.astype(jnp.float32) + water_driving_term).astype(jnp.bfloat16)
    table = jnp.asarray(lon_table(NLON))
    warmth_by_lat = lax.all_to_all(
        water_warmth_on_air_grid.astype(jnp.bfloat16), "col", split_axis=0, concat_axis=1, tiled=True
    )
    driving_by_lat = jnp.einsum(
        "tjf,fc->tjc", warmth_by_lat, interface_driving_matrix, preferred_element_type=jnp.float32
    )
    by_lat = (air_by_lat.astype(jnp.float32) + driving_by_lat).astype(jnp.bfloat16)
    spectra = jnp.einsum("tjc,jk->tkc", by_lat, table, preferred_element_type=jnp.float32).astype(
        jnp.bfloat16
    )
    columns = lax.all_to_all(spectra, ("row", "col"), split_axis=1, concat_axis=0, tiled=True)
    modes = jnp.einsum(
        "tkc,klt->klc", columns, forward_basis, preferred_element_type=jnp.float32
    ).astype(jnp.bfloat16)
    mixed = mix_direct(modes, mixing_weight)
    mixed = (mixed * degree_filter[None]).astype(jnp.bfloat16)
    synth = jnp.einsum(
        "kld,ktl->tkd", mixed, inverse_basis, preferred_element_type=jnp.float32
    ).astype(jnp.bfloat16)
    rejoined = lax.all_to_all(synth, ("row", "col"), split_axis=0, concat_axis=1, tiled=True)
    grid = jnp.einsum("tkd,jk->tjd", rejoined, table, preferred_element_type=jnp.float32).astype(
        jnp.bfloat16
    )
    grid_home = lax.all_to_all(grid, "col", split_axis=1, concat_axis=0, tiled=True)
    atm_out = (lifted.astype(jnp.float32) + jax.nn.gelu(grid_home.astype(jnp.float32))).astype(
        jnp.bfloat16
    )
    hidden = jax.nn.gelu(conv_taps(channels(widen(water_condition)), first_ocean_kernel)).astype(
        jnp.bfloat16
    )
    inner = conv_taps(channels(widen(hidden)), second_ocean_kernel)
    lift = jnp.dot(
        flux_ocean, flux_lift_weight.astype(jnp.float32), precision=lax.Precision.HIGHEST
    )
    mask_values = ocean_cell_mask.astype(jnp.float32)[:, :, None]
    ocean_out = (water_condition.astype(jnp.float32) + mask_values * (inner + lift)).astype(
        jnp.bfloat16
    )
    return (atm_out, ocean_out)


def solution(mesh):
    placed = (
        P("row", "col", "comp"),
        P("row", "col", "comp"),
        P("row", "col"),
        P("row", "col", None),
        P("row", "col", None),
        P("row", "col", None),
        P("row", "col", None),
        P("comp", None),
        P(None, "comp"),
        P("comp", None),
        P(None, "comp"),
        P(("row", "col"), None, None),
        P(("row", "col"), None, None),
        P(None, "comp"),
        P(None, "comp"),
        P(None, None, None, "comp"),
        P(None, None, None, "comp"),
    )
    return jax.shard_map(
        local,
        mesh=mesh,
        in_specs=placed,
        out_specs=(P("row", "col", "comp"), P("row", "col", "comp")),
        check_vma=False,
    )
```

```python
import math

import jax
import jax.numpy as jnp
import ml_dtypes
import numpy as np
from jax import lax
from jax.experimental import pallas as pl
from jax.experimental.pallas import tpu as pltpu
from jax.sharding import PartitionSpec as P

BF16 = jnp.bfloat16
F32 = jnp.float32
MESH = pl.DeviceIdType.MESH
LANES = 256


def lon_table(count):
    col_idx = np.arange(count, dtype=np.int64)[:, None]
    coef_idx = np.arange(count, dtype=np.int64)[None, :]
    half_count = count // 2
    freq = np.where(coef_idx <= half_count, coef_idx, coef_idx - half_count)
    phase = (col_idx * freq % count) * (2.0 * math.pi / count)
    values = np.where(coef_idx <= half_count, np.cos(phase), np.sin(phase))
    return (values * math.sqrt(2.0 / count)).astype(ml_dtypes.bfloat16)


def dot(a, b):
    return jnp.dot(a, b, preferred_element_type=F32)


def dot_nt(a, b):
    return lax.dot_general(a, b, (((1,), (1,)), ((), ())), preferred_element_type=F32)


def dot_tn(a, b):
    return lax.dot_general(a, b, (((0,), (0,)), ((), ())), preferred_element_type=F32)


def drain(ref, sem):
    pltpu.make_async_copy(ref, ref, sem).wait()


def gelu(x):
    return jax.nn.gelu(x, approximate=True)


def make_kernel(NR, NC, NX, PT, PM, C, WY, WX, CO, NF, DEG):
    LT = PT // NC
    NLON = NC * PM
    ND = NR * NC
    KB = NLON // ND
    NLAT = NR * PT
    NY = NC // NX
    AR, AC = PT + 2, PM + 2
    OR, OC = WY + 2, WX + 2
    WP = WX + 16
    XR = WY + 4
    HR_ = WY + 2
    FB = NLON // 4

    def kernel(
        atm, water, mask, oidx, ow, aidx, aw, fwt, flw, ipmt, drv, fb_h, ib_h, mw_h, filt_h, k1_h, k2_h,
        tab_h, tabt_h, atm_out, ocean_out,
        atm_v, g1, tabt, tab, sp, rx, rxf, fb, ib, md, mp, mw, filt, qf, qb, vx, bx, gs, hh, lf,
        x, hl, hr, hd, w1, w2, oo, dsc,
        tf, ts, pf, ps, ef, es, efl, efr, esl, esr, rsc, csc, wsc, ss, sr, fx,
        ld, wsend, wrecv, csend, crecv, hsend, hrecv, g1s, g1r, sss, ssr, s2s, r2, mds, mdr,
        q_s, q_r, gss, gsr, hds, hdr, outs, ready,
    ):
        me = lax.axis_index("comp")
        row = lax.axis_index("row")
        col = lax.axis_index("col")
        flat = row * NC + col
        other = 1 - me

        def rmod(v):
            return lax.rem(v + NR, NR)

        def cmod(v):
            return lax.rem(v + NC, NC)

        def shifted(py, px):
            y = lax.rem(col // NX + py, NY)
            xx = lax.rem(lax.rem(col, NX) + px, NX)
            return y * NX + xx

        def send(src, dst, ssem, rsem, dev):
            pltpu.make_async_remote_copy(
                src_ref=src, dst_ref=dst, send_sem=ssem, recv_sem=rsem, device_id=dev, device_id_type=MESH
            ).start()

        def load(i, src, dst):
            pltpu.make_async_copy(src, dst, ld.at[i]).start()

        barrier = pltpu.get_barrier_semaphore()

        def greet(dev):
            pl.semaphore_signal(barrier, inc=1, device_id=dev, device_id_type=MESH)

        for d in range(1, NC):
            greet((me, row, cmod(col + d)))
        for d in range(1, NR):
            greet((me, rmod(row + d), col))
        for dr in (-1, 0, 1):
            for dc in (-1, 0, 1):
                greet((other, rmod(row + dr), cmod(col + dc)))
                if dr and dc:
                    greet((me, rmod(row + dr), cmod(col + dc)))

        load(0, atm, atm_v)
        load(1, water, x.at[me, 2 : 2 + WY, 0:WX])
        load(2, tabt_h, tabt)
        load(3, fb_h, fb)
        load(4, ib_h, ib)
        load(5, mw_h, mw)
        load(6, filt_h, filt)
        load(7, tab_h, tab)
        for a in range(3):
            for b in range(3):
                rows = pl.ds(a * 2 * CO, 2 * CO)
                cols = pl.ds(b * CO, CO)
                pltpu.make_async_copy(k1_h.at[a, b], w1.at[rows, cols], ld.at[8]).start()
                pltpu.make_async_copy(k2_h.at[a, b], w2.at[rows, cols], ld.at[9]).start()

        pl.semaphore_wait(barrier, NC - 1 + NR - 1 + 9 + 4)
        for d in range(1, NR):
            pl.semaphore_signal(ready, inc=1, device_id=(me, rmod(row + d), col), device_id_type=MESH)

        def send_lat(t):
            pltpu.make_async_copy(atm.at[col * LT + t], g1.at[t, pl.ds(col * PM, PM)], g1r.at[t]).start()

            def step(p, _):
                there = shifted(p // NX, lax.rem(p, NX))
                send(
                    atm.at[there * LT + t], g1.at[t, pl.ds(col * PM, PM)], g1s.at[t], g1r.at[t], (me, row, there)
                )
                return 0

            lax.fori_loop(1, NC, step, 0)

        def water_sends(q):
            return [
                (row > 0, water.at[0:2], x.at[me, XR - 2 : XR, 0:WX], (q, rmod(row - 1), col)),
                (row < NR - 1, water.at[WY - 2 : WY], x.at[me, 0:2, 0:WX], (q, rmod(row + 1), col)),
                (col > 0, water.at[:, 0:16], hr.at[me, 2 : 2 + WY], (q, row, cmod(col - 1))),
                (col < NC - 1, water.at[:, WX - 16 : WX], hl.at[me, 2 : 2 + WY], (q, row, cmod(col + 1))),
                ((row > 0) & (col > 0), water.at[0:2, 0:16], hr.at[me, XR - 2 : XR],
                 (q, rmod(row - 1), cmod(col - 1))),
                ((row > 0) & (col < NC - 1), water.at[0:2, WX - 16 : WX], hl.at[me, XR - 2 : XR],
                 (q, rmod(row - 1), cmod(col + 1))),
                ((row < NR - 1) & (col > 0), water.at[WY - 2 : WY, 0:16], hr.at[me, 0:2],
                 (q, rmod(row + 1), cmod(col - 1))),
                ((row < NR - 1) & (col < NC - 1), water.at[WY - 2 : WY, WX - 16 : WX], hl.at[me, 0:2],
                 (q, rmod(row + 1), cmod(col + 1))),
            ]

        def water_recvs(q):
            return [
                (row < NR - 1, x.at[q, XR - 2 : XR, 0:WX]),
                (row > 0, x.at[q, 0:2, 0:WX]),
                (col < NC - 1, hr.at[q, 2 : 2 + WY]),
                (col > 0, hl.at[q, 2 : 2 + WY]),
                ((row < NR - 1) & (col < NC - 1), hr.at[q, XR - 2 : XR]),
                ((row < NR - 1) & (col > 0), hl.at[q, XR - 2 : XR]),
                ((row > 0) & (col < NC - 1), hr.at[q, 0:2]),
                ((row > 0) & (col > 0), hl.at[q, 0:2]),
            ]

        send_lat(0)

        drain(x.at[0, 2 : 2 + WY, 0:WX], ld.at[1])
        wv = x.at[me]

        def project_water(i, _):
            cells = wv[pl.ds(2 + 4 * i, 4), 0:WX, :].reshape(4 * WX, CO)
            got = dot_nt(ipmt[...], cells).astype(BF16)
            for j in range(4):
                ps[me, pl.ds((4 * i + j) * NF, NF), :] = got[:, j * WX : (j + 1) * WX]
            return 0

        lax.fori_loop(0, WY // 4, project_water, 0)
        send(ps.at[me], ps.at[me], csend.at[0], crecv.at[0], (other, row, col))

        drain(atm_v, ld.at[0])

        def project_air(t, _):
            cells = atm_v[pl.ds(t * 4, 4)].reshape(4 * PM, C)
            got = dot_nt(fwt[...], cells)
            zeros = jnp.zeros((NF, 128 - PM), F32)
            for j in range(4):
                part = jnp.concatenate([got[:, j * PM : (j + 1) * PM], zeros], axis=1)
                pf[me, pl.ds((t * 4 + j) * NF, NF), :] = part.astype(BF16)
            return 0

        lax.fori_loop(0, PT // 4, project_air, 0)
        send(pf.at[me], pf.at[me], csend.at[1], crecv.at[1], (other, row, col))

        def both(part):
            return (part[0].astype(F32) + part[1].astype(F32)).astype(BF16)

        lane = lax.broadcasted_iota(jnp.int32, (16, 128), 1)
        line = lax.broadcasted_iota(jnp.int32, (16, 128), 0)

        def pick(cond):
            return jnp.where(cond, 1.0, 0.0).astype(BF16)

        def row_halo(tab_ref, rows, at):
            above = pl.ds((rows + 1) * NF, NF)
            below = pl.ds(rows * NF, NF)

            @pl.when(row > 0)
            def _():
                send(tab_ref.at[0:NF, 0:128], tab_ref.at[below, 0:128], hsend.at[at], hrecv.at[at],
                     (me, rmod(row - 1), col))

            @pl.when(row < NR - 1)
            def _():
                send(tab_ref.at[(rows - 1) * NF : rows * NF, 0:128], tab_ref.at[above, 0:128],
                     hsend.at[at + 1], hrecv.at[at + 1], (me, rmod(row + 1), col))

            @pl.when(row < NR - 1)
            def _():
                drain(tab_ref.at[below, 0:128], hrecv.at[at])

            @pl.when(row == NR - 1)
            def _():
                tab_ref[below, 0:128] = jnp.zeros((NF, 128), BF16)

            @pl.when(row > 0)
            def _():
                drain(tab_ref.at[above, 0:128], hrecv.at[at + 1])

            @pl.when(row == 0)
            def _():
                tab_ref[above, 0:128] = jnp.zeros((NF, 128), BF16)

        def sent(cond, ref, at):
            @pl.when(cond)
            def _():
                drain(ref, hsend.at[at])

        def row_halo_sent(tab_ref, at):
            sent(row > 0, tab_ref.at[0:NF, 0:128], at)
            sent(row < NR - 1, tab_ref.at[0:NF, 0:128], at + 1)

        def col_halo_send(tab_ref, edge, left, right, width, at):
            ends = pick(((line == 0) & (lane == 0)) | ((line == 1) & (lane == width - 1)))
            edge[...] = dot_nt(ends, tab_ref[:, 0:128]).astype(BF16)

            @pl.when(col > 0)
            def _():
                send(edge, right, hsend.at[at], hrecv.at[at], (me, row, cmod(col - 1)))

            @pl.when(col < NC - 1)
            def _():
                send(edge, left, hsend.at[at + 1], hrecv.at[at + 1], (me, row, cmod(col + 1)))

        def col_halo_recv(left, right, at):
            @pl.when(col < NC - 1)
            def _():
                drain(right, hrecv.at[at])

            @pl.when(col == NC - 1)
            def _():
                right[...] = jnp.zeros(right.shape, BF16)

            @pl.when(col > 0)
            def _():
                drain(left, hrecv.at[at + 1])

            @pl.when(col == 0)
            def _():
                left[...] = jnp.zeros(left.shape, BF16)

        def halo_columns(left, right, place):
            from_right = pick((line == 0) & (lane == place))
            from_left = pick((line == 1) & (lane == place + 1))
            return dot_tn(right[...], from_right) + dot_tn(left[...], from_left)

        def regrid(tab_ref, index, weight, rows, cols, block):
            cells = index.astype(F32)
            r_at = jnp.floor((cells + 0.5) * (1.0 / cols))
            c_at = cells - r_at * cols
            rsc[...] = jnp.where(r_at == 0, rows - 1.0, r_at - 1.0)
            csc[...] = jnp.where(c_at == 0, cols - 1.0, c_at - 1.0)
            wsc[...] = weight / jnp.sum(weight, axis=0, keepdims=True)
            width = tab_ref.shape[1]
            at = lax.broadcasted_iota(jnp.int32, (width, LANES), 0).astype(F32)

            def source(k, total):
                r_k = rsc[pl.ds(k, 1), :]
                c_k = csc[pl.ds(k, 1), :]
                w_k = wsc[pl.ds(k, 1), :]
                chosen = jnp.where(at == c_k, 1.0, 0.0).astype(BF16)
                for b in range(rows // block):
                    lines = dot(tab_ref[b * block * NF : (b + 1) * block * NF, :], chosen)
                    for j in range(block):
                        share = jnp.where(r_k == float(b * block + j), w_k, 0.0)
                        total = total + lines[j * NF : (j + 1) * NF] * share
                return total

            return lax.fori_loop(0, 4, source, jnp.zeros((NF, LANES), F32))

        drain(ps.at[0], crecv.at[0])
        ts[0 : WY * NF, 0:128] = both(ps)
        row_halo(ts, WY, 0)
        col_halo_send(ts, es, esl, esr, WX, 4)
        send_lat(1)
        for q in range(2):
            for n, (there, src, dst, dev) in enumerate(water_sends(q)):
                @pl.when(there)
                def _(src=src, dst=dst, dev=dev, n=n, q=q):
                    send(src, dst, wsend.at[n, q], wrecv.at[n, me], dev)
        send(water, x.at[me, 2 : 2 + WY, 0:WX], wsend.at[8, 0], wrecv.at[8, 0], (other, row, col))
        send_lat(2)

        drain(pf.at[0], crecv.at[1])
        tf[0 : PT * NF, :] = both(pf)
        row_halo(tf, PT, 2)
        col_halo_send(tf, ef, efl, efr, PM, 6)

        col_halo_recv(esl, esr, 4)
        row_halo_sent(ts, 0)
        ts[:, 128:256] = halo_columns(esl, esr, 0).astype(BF16)

        def to_air(c, _):
            idx = jnp.concatenate(
                [aidx[c * LT + i] for i in range(LT)] + [jnp.zeros((4, LANES - LT * PM), jnp.int32)], axis=1
            )
            wgt = jnp.concatenate(
                [aw[c * LT + i] for i in range(LT)] + [jnp.ones((4, LANES - LT * PM), F32)], axis=1
            )
            ss[c] = regrid(ts, idx, wgt, OR, OC, 13 if OR % 13 == 0 else 1).astype(BF16)

            @pl.when(c != col)
            def _():
                send(ss.at[c], sr.at[col], sss, ssr, (me, row, c))

            return 0

        lax.fori_loop(0, NC, to_air, 0)
        pltpu.make_async_copy(ss.at[col], sr.at[col], ssr).start()

        def lift_here(c, _):
            term = dot_tn(ss[c], drv[...])
            for i in range(LT):
                t = c * LT + i
                lf[t] = (atm_v[t].astype(F32) + term[i * PM : (i + 1) * PM]).astype(BF16)
            return 0

        lax.fori_loop(0, NC, lift_here, 0)

        drain(sr, ssr)

        def lift_terms(c, _):
            dsc[c] = dot_tn(sr[c], drv[...])
            return 0

        lax.fori_loop(0, NC, lift_terms, 0)

        drain(tabt, ld.at[2])
        pl.semaphore_wait(ready, NR - 1)

        for t in range(LT):
            drain(g1.at[t], g1r.at[t])

            def lift_lat(c, _, t=t):
                rows = pl.ds(pl.multiple_of(c * PM, PM), PM)
                g1[t, rows, :] = (
                    g1[t, rows, :].astype(F32) + dsc[c, t * PM : (t + 1) * PM, :]
                ).astype(BF16)
                return 0

            lax.fori_loop(0, NC, lift_lat, 0)

            def analyse(b, _, t=t):
                rows = pl.ds(pl.multiple_of(b * FB, FB), FB)
                got = dot(tabt[rows, :], g1[t])
                halves = [got[:, h * 128 : (h + 1) * 128].reshape(FB // 8, 8, 128) for h in range(2)]
                sp[t, pl.ds(b * (FB // 8), FB // 8)] = jnp.concatenate(halves, axis=1).astype(BF16)
                return 0

            lax.fori_loop(0, 4, analyse, 0)
            pltpu.make_async_copy(sp.at[t, flat], rx.at[flat * LT + t], r2.at[t]).start()

            def scatter(p, _, t=t):
                r_to = rmod(row + p // NC)
                c_to = shifted(lax.rem(p, NC) // NX, lax.rem(p, NX))
                send(sp.at[t, r_to * NC + c_to], rx.at[flat * LT + t], s2s.at[t], r2.at[t], (me, r_to, c_to))
                return 0

            lax.fori_loop(1, ND, scatter, 0)

        for q in range(2):
            for n, (there, dst) in enumerate(water_recvs(q)):
                @pl.when(there)
                def _(dst=dst, n=n, q=q):
                    drain(dst, wrecv.at[n, q])
        drain(x.at[0, 2 : 2 + WY, 0:WX], wrecv.at[8, 0])

        @pl.when(row == 0)
        def _():
            x[:, 0:2, 0:WX, :] = jnp.zeros((2, 2, WX, CO), BF16)

        @pl.when(row == NR - 1)
        def _():
            x[:, XR - 2 : XR, 0:WX, :] = jnp.zeros((2, 2, WX, CO), BF16)

        def side(i, _):
            inside = ((i >= 2) | (row > 0)) & ((i < XR - 2) | (row < NR - 1))
            sub = lax.broadcasted_iota(jnp.int32, (16, CO), 0)
            for q in range(2):
                from_right = jnp.where((sub < 2) & inside & (col < NC - 1), hr[q, i].astype(F32), 0.0)
                from_left = jnp.where((sub >= 14) & inside & (col > 0), hl[q, i].astype(F32), 0.0)
                x[q, i, WX:WP, :] = (from_right + from_left).astype(BF16)
            return 0

        lax.fori_loop(0, XR, side, 0)
        drain(w1, ld.at[8])

        def taps(src, weight, first, count):
            lhs = jnp.concatenate(
                [
                    jnp.concatenate([src[q, first + j + a] for a in range(3) for q in range(2)], axis=1)
                    for j in range(count)
                ],
                axis=0,
            )
            got = dot(lhs, weight[...])
            outs_ = []
            for j in range(count):
                part = got[j * WP : (j + 1) * WP]
                outs_.append(
                    pltpu.roll(part[:, 0:CO], 1, 0)
                    + part[:, CO : 2 * CO]
                    + pltpu.roll(part[:, 2 * CO : 3 * CO], WP - 1, 0)
                )
            return outs_

        def conv_first(i, _):
            place = lax.broadcasted_iota(jnp.int32, (WP, CO), 0)
            edge = ((place == WP - 1) & (col == 0)) | ((place == WX) & (col == NC - 1))
            for j, out in enumerate(taps(x, w1, 2 * i, 2)):
                h = 2 * i + j
                outside = ((h == 0) & (row == 0)) | ((h == HR_ - 1) & (row == NR - 1))
                hd[me, h] = jnp.where(edge | outside, 0.0, gelu(out)).astype(BF16)
            return 0

        lax.fori_loop(0, HR_ // 2, conv_first, 0)
        send(hd.at[me], hd.at[me], hds, hdr, (other, row, col))

        col_halo_recv(efl, efr, 6)
        row_halo_sent(tf, 2)
        tf[...] = (tf[...].astype(F32) + halo_columns(efl, efr, PM)).astype(BF16)

        def to_ocean(i, _):
            idx = jnp.concatenate([oidx[2 * i], oidx[2 * i + 1]], axis=1)
            wgt = jnp.concatenate([ow[2 * i], ow[2 * i + 1]], axis=1)
            fx[i] = regrid(tf, idx, wgt, AR, AC, 10 if AR % 10 == 0 else 1).astype(BF16)
            return 0

        lax.fori_loop(0, WY // 2, to_ocean, 0)

        drain(hd.at[0], hdr)
        drain(w2, ld.at[9])

        def conv_second(i, _):
            outs_ = taps(hd, w2, 2 * i, 2)
            sixteenth = jnp.full((NF, CO), 1.0 / NF, BF16)
            for j in range(2):
                r = 2 * i + j
                lift = dot_tn(fx[i, :, j * WX : (j + 1) * WX], flw[...])
                line_mask = jnp.broadcast_to(mask[pl.ds(r, 1), :].astype(F32), (NF, WX)).astype(BF16)
                keep = dot_tn(line_mask, sixteenth)
                here = x[me, r + 2, 0:WX, :].astype(F32)
                oo[r] = (here + keep * (outs_[j][0:WX] + lift)).astype(BF16)
            return 0

        lax.fori_loop(0, WY // 2, conv_second, 0)
        pltpu.make_async_copy(oo, ocean_out, outs.at[0]).start()

        drain(fb, ld.at[3])
        for t in range(LT):
            drain(rx.at[0:ND], r2.at[t])
        TB = 32 if NLAT % 32 == 0 else 8

        def widen(i, _):
            rows = pl.ds(pl.multiple_of(i * TB, TB), TB)
            out_rows = pl.ds(pl.multiple_of(i * TB * 16, TB * 16), TB * 16)
            rxf[out_rows, :] = rx[rows].astype(F32).reshape(TB * 16, 128)
            return 0

        lax.fori_loop(0, NLAT // TB, widen, 0)

        def to_modes(k, _):
            col_k = jnp.concatenate(
                [rxf[pl.ds(k + 8 * h, NLAT, stride=16), :] for h in range(2)], axis=1
            ).astype(BF16)
            md[k] = dot(fb[k], col_k).astype(BF16)
            send(md.at[k], mp.at[k], mds.at[k], mdr.at[k], (other, row, col))
            return 0

        lax.fori_loop(0, KB, to_modes, 0)
        drain(ib, ld.at[4])
        drain(mw, ld.at[5])
        drain(filt, ld.at[6])

        def to_synth(k, _):
            drain(mp.at[k], mdr.at[k])
            mixed = dot(md[k], mw[pl.ds(pl.multiple_of(me * C, C), C), :])
            mixed = mixed + dot(mp[k], mw[pl.ds(pl.multiple_of(other * C, C), C), :])
            mixed = (mixed * filt[...]).astype(BF16)
            got = dot(ib[k], mixed)
            for h in range(2):
                qf[pl.ds(k + 8 * h, NLAT, stride=16), :] = got[:, h * 128 : (h + 1) * 128]
            return 0

        lax.fori_loop(0, KB, to_synth, 0)

        def narrow(i, _):
            rows = pl.ds(pl.multiple_of(i * TB, TB), TB)
            in_rows = pl.ds(pl.multiple_of(i * TB * 16, TB * 16), TB * 16)
            qb[rows] = qf[in_rows, :].reshape(TB, 16, 128).astype(BF16)
            return 0

        lax.fori_loop(0, NLAT // TB, narrow, 0)

        for t in range(LT):
            pltpu.make_async_copy(qb.at[flat * LT + t], vx.at[t, flat], q_r.at[t]).start()

            def gather_back(p, _, t=t):
                r_to = rmod(row + p // NC)
                c_to = shifted(lax.rem(p, NC) // NX, lax.rem(p, NX))
                send(
                    qb.at[(r_to * NC + c_to) * LT + t], vx.at[t, flat], q_s.at[t], q_r.at[t], (me, r_to, c_to)
                )
                return 0

            lax.fori_loop(1, ND, gather_back, 0)

        drain(tab, ld.at[7])
        for t in range(LT):
            drain(vx.at[t], q_r.at[t])
            for h in range(2):
                part = vx[t].astype(F32)[:, 8 * h : 8 * h + 8, :].reshape(NLON, 128)
                bx[:, h * 128 : (h + 1) * 128] = part.astype(BF16)

            def synthesise(b, _, t=t):
                rows = pl.ds(pl.multiple_of(b * FB, FB), FB)
                gs[t, rows, :] = dot(tab[rows, :], bx[...]).astype(BF16)
                return 0

            lax.fori_loop(0, 4, synthesise, 0)
            pltpu.make_async_copy(
                gs.at[t, pl.ds(col * PM, PM)], hh.at[col * LT + t], gsr.at[t]
            ).start()

            def home(p, _, t=t):
                there = shifted(p // NX, lax.rem(p, NX))
                send(
                    gs.at[t, pl.ds(there * PM, PM)], hh.at[col * LT + t], gss.at[t], gsr.at[t], (me, row, there)
                )
                return 0

            lax.fori_loop(1, NC, home, 0)

        for t in range(LT):
            drain(hh.at[0:NC], gsr.at[t])

            def finish(c, _, t=t):
                i = c * LT + t
                lf[i] = (lf[i].astype(F32) + gelu(hh[i].astype(F32))).astype(BF16)
                return 0

            lax.fori_loop(0, NC, finish, 0)
        pltpu.make_async_copy(lf, atm_out, outs.at[1]).start()

        for t in range(LT):
            drain(g1.at[t, 0 : (NC - 1) * PM], g1s.at[t])
            drain(sp.at[t, 0 : ND - 1], s2s.at[t])
            drain(vx.at[t, 0 : ND - 1], q_s.at[t])
            drain(gs.at[t, 0 : (NC - 1) * PM], gss.at[t])
        drain(sr.at[0 : NC - 1], sss)
        for q in range(2):
            for n, (there, src, dst, dev) in enumerate(water_sends(q)):
                @pl.when(there)
                def _(src=src, n=n, q=q):
                    drain(src, wsend.at[n, q])
        drain(water, wsend.at[8, 0])
        drain(ps.at[0], csend.at[0])
        drain(pf.at[0], csend.at[1])
        drain(hd.at[0], hds)
        for k in range(KB):
            drain(mp.at[k], mds.at[k])
        for at, edge in ((4, es), (6, ef)):
            sent(col > 0, edge, at)
            sent(col < NC - 1, edge, at + 1)
        drain(oo, outs.at[0])
        drain(lf, outs.at[1])

    v = pltpu.VMEM
    dma = pltpu.SemaphoreType.DMA
    scratch = [
        v((PT, PM, C), BF16), v((LT, NLON, C), BF16), v((NLON, NLON), BF16), v((NLON, NLON), BF16),
        v((LT, ND, 16, 128), BF16), v((NLAT, 16, 128), BF16), v((NLAT * 16, 128), F32),
        v((KB, DEG, NLAT), BF16), v((KB, NLAT, DEG), BF16), v((KB, DEG, C), BF16), v((KB, DEG, C), BF16),
        v((2 * C, C), BF16), v((DEG, C), F32), v((NLAT * 16, 128), F32), v((NLAT, 16, 128), BF16),
        v((LT, ND, 16, 128), BF16), v((NLON, C), BF16), v((LT, NLON, C), BF16), v((PT, PM, C), BF16),
        v((PT, PM, C), BF16),
        v((2, XR, WP, CO), BF16), v((2, XR, 16, CO), BF16), v((2, XR, 16, CO), BF16), v((2, HR_, WP, CO), BF16),
        v((6 * CO, 3 * CO), BF16), v((6 * CO, 3 * CO), BF16), v((WY, WX, CO), BF16),
        v((NC, LANES, C), F32),
        v((AR * NF, 128), BF16), v((OR * NF, 256), BF16), v((2, PT * NF, 128), BF16), v((2, WY * NF, 128), BF16),
        v((16, AR * NF), BF16), v((16, OR * NF), BF16),
        v((16, AR * NF), BF16), v((16, AR * NF), BF16), v((16, OR * NF), BF16), v((16, OR * NF), BF16),
        v((4, LANES), F32), v((4, LANES), F32), v((4, LANES), F32),
        v((NC, NF, LANES), BF16), v((NC, NF, LANES), BF16), v((WY // 2, NF, LANES), BF16),
        dma((10,)), dma((9, 2)), dma((9, 2)), dma((2,)), dma((2,)), dma((8,)), dma((8,)),
        dma((LT,)), dma((LT,)), dma, dma, dma((LT,)), dma((LT,)), dma((KB,)), dma((KB,)),
        dma((LT,)), dma((LT,)), dma((LT,)), dma((LT,)), dma, dma, dma((2,)), pltpu.SemaphoreType.REGULAR,
    ]
    any_ = pl.BlockSpec(memory_space=pl.ANY)
    vm = pl.BlockSpec(memory_space=pltpu.VMEM)
    return pl.pallas_call(
        kernel,
        out_shape=(
            jax.ShapeDtypeStruct((PT, PM, C), BF16),
            jax.ShapeDtypeStruct((WY, WX, CO), BF16),
        ),
        in_specs=[any_, any_] + [vm] * 9 + [any_] * 8,
        out_specs=(any_, any_),
        scratch_shapes=scratch,
        compiler_params=pltpu.CompilerParams(
            collective_id=0, has_side_effects=True, vmem_limit_bytes=60 * 1024 * 1024
        ),
        cost_estimate=pl.CostEstimate(flops=9_000_000_000, bytes_accessed=20_000_000, transcendentals=2_000_000),
        name="coupled_step",
    )


def solution(mesh):
    NR, NC = mesh.shape["row"], mesh.shape["col"]
    NX = 4 if NC == 16 else NC

    def local(
        atmosphere_state, water_condition, ocean_cell_mask, atmos_to_ocean_index, atmos_to_ocean_weight,
        water_source_positions, water_source_overlay_areas, flux_weight, flux_lift_weight,
        interface_projection_matrix, interface_driving_matrix, forward_basis, inverse_basis,
        mixing_weight, degree_filter, first_ocean_kernel, second_ocean_kernel,
    ):
        PT, PM, C = atmosphere_state.shape
        WY, WX, CO = water_condition.shape
        table = lon_table(NC * PM)
        step = make_kernel(
            NR, NC, NX, PT, PM, C, WY, WX, CO, flux_weight.shape[1], forward_basis.shape[1]
        )
        return step(
            atmosphere_state,
            water_condition,
            ocean_cell_mask,
            jnp.swapaxes(atmos_to_ocean_index, 1, 2),
            jnp.swapaxes(atmos_to_ocean_weight, 1, 2),
            jnp.swapaxes(water_source_positions, 1, 2),
            jnp.swapaxes(water_source_overlay_areas, 1, 2),
            flux_weight.T,
            flux_lift_weight,
            interface_projection_matrix.T,
            interface_driving_matrix,
            forward_basis,
            inverse_basis,
            mixing_weight,
            degree_filter,
            first_ocean_kernel,
            second_ocean_kernel,
            jnp.asarray(table),
            jnp.asarray(np.ascontiguousarray(table.T)),
        )

    placed = (
        P("row", "col", "comp"),
        P("row", "col", "comp"),
        P("row", "col"),
        P("row", "col", None),
        P("row", "col", None),
        P("row", "col", None),
        P("row", "col", None),
        P("comp", None),
        P(None, "comp"),
        P("comp", None),
        P(None, "comp"),
        P(("row", "col"), None, None),
        P(("row", "col"), None, None),
        P(None, "comp"),
        P(None, "comp"),
        P(None, None, None, "comp"),
        P(None, None, None, "comp"),
    )
    return jax.shard_map(
        local,
        mesh=mesh,
        in_specs=placed,
        out_specs=(P("row", "col", "comp"), P("row", "col", "comp")),
        check_vma=False,
    )
```

```python
import math

import jax
import jax.numpy as jnp
import ml_dtypes
import numpy as np
from jax import lax
from jax.experimental import pallas as pl
from jax.experimental.pallas import tpu as pltpu
from jax.sharding import PartitionSpec as P

BF16 = jnp.bfloat16
F32 = jnp.float32
MESH = pl.DeviceIdType.MESH
LANES = 256


def lon_table(count):
    col_idx = np.arange(count, dtype=np.int64)[:, None]
    coef_idx = np.arange(count, dtype=np.int64)[None, :]
    half_count = count // 2
    freq = np.where(coef_idx <= half_count, coef_idx, coef_idx - half_count)
    phase = (col_idx * freq % count) * (2.0 * math.pi / count)
    values = np.where(coef_idx <= half_count, np.cos(phase), np.sin(phase))
    return (values * math.sqrt(2.0 / count)).astype(ml_dtypes.bfloat16)


def dot(a, b):
    return jnp.dot(a, b, preferred_element_type=F32)


def dot_nt(a, b):
    return lax.dot_general(a, b, (((1,), (1,)), ((), ())), preferred_element_type=F32)


def dot_tn(a, b):
    return lax.dot_general(a, b, (((0,), (0,)), ((), ())), preferred_element_type=F32)


def drain(ref, sem):
    pltpu.make_async_copy(ref, ref, sem).wait()


def gelu(x):
    return jax.nn.gelu(x, approximate=True)


def make_kernel(NR, NC, NX, PT, PM, C, WY, WX, CO, NF, DEG):
    LT = PT // NC
    NLON = NC * PM
    ND = NR * NC
    KB = NLON // ND
    NLAT = NR * PT
    NY = NC // NX
    HC, HO = NC // 2, WY // 4
    AR, AC = PT + 2, PM + 2
    OR, OC = WY + 2, WX + 2
    WP = WX + 16
    XR = WY + 4
    HR_ = WY + 2
    FB = NLON // 4

    def kernel(
        atm, water, mask_h, oidx_h, ow_h, aidx_h, aw_h, fwt_h, flw_h, ipmt_h, drv_h, fb_h, ib_h, mw_h, filt_h,
        k1_h, k2_h, tab_h, tabt_h, lifted_out, grid_out, ocean_out,
        mask, oidx, ow, aidx, aw, fwt, flw, ipmt, drv,
        atm_v, g1, tabt, tab, sp, rx, rxf, fb, ib, md, mp, mw, filt, qf, qb, vx, bx, gs, lf, fbp, acc, ms,
        x, hl, hr, hd, w1, w2, oo, dsc,
        tf, ts, pf, ps, ef, es, efl, efr, esl, esr, rsc, csc, wsc, ss, sr, fx,
        ld, wsend, wrecv, csend, crecv, hsend, hrecv, g1s, g1r, sss, ssr, s2s, r2, mds, mdr,
        q_s, q_r, gss, gsr, hds, hdr, outs, shs, shr, fxs, fxr, ready,
    ):
        me = lax.axis_index("comp")
        row = lax.axis_index("row")
        col = lax.axis_index("col")
        flat = row * NC + col
        other = 1 - me

        def rmod(v):
            return lax.rem(v + NR, NR)

        def cmod(v):
            return lax.rem(v + NC, NC)

        def shifted(py, px):
            y = lax.rem(col // NX + py, NY)
            xx = lax.rem(lax.rem(col, NX) + px, NX)
            return y * NX + xx

        def partner(p):
            return rmod(row + lax.rem(p, NR)), shifted(p // (NR * NX), lax.rem(p // NR, NX))

        def send(src, dst, ssem, rsem, dev):
            pltpu.make_async_remote_copy(
                src_ref=src, dst_ref=dst, send_sem=ssem, recv_sem=rsem, device_id=dev, device_id_type=MESH
            ).start()

        def load(i, src, dst):
            pltpu.make_async_copy(src, dst, ld.at[i]).start()

        barrier = pltpu.get_barrier_semaphore()

        def greet(dev):
            pl.semaphore_signal(barrier, inc=1, device_id=dev, device_id_type=MESH)

        for d in range(1, NC):
            greet((me, row, cmod(col + d)))
        for d in range(1, NR):
            greet((me, rmod(row + d), col))
        for dr in (-1, 0, 1):
            for dc in (-1, 0, 1):
                greet((other, rmod(row + dr), cmod(col + dc)))
                if dr and dc:
                    greet((me, rmod(row + dr), cmod(col + dc)))

        load(1, water, x.at[me, 2 : 2 + WY, 0:WX])
        load(10, ipmt_h, ipmt)
        load(0, atm, atm_v)
        for n, (src, dst) in enumerate(
            ((fwt_h, fwt), (aidx_h, aidx), (aw_h, aw), (drv_h, drv), (mask_h, mask), (oidx_h, oidx), (ow_h, ow),
             (flw_h, flw))
        ):
            load(11 + n, src, dst)
        load(2, tabt_h, tabt)
        load(3, fb_h, fb)
        for a in range(3):
            for b in range(3):
                rows = pl.ds(a * 2 * CO, 2 * CO)
                cols = pl.ds(b * CO, CO)
                pltpu.make_async_copy(k1_h.at[a, b], w1.at[rows, cols], ld.at[8]).start()
                pltpu.make_async_copy(k2_h.at[a, b], w2.at[rows, cols], ld.at[9]).start()
        load(5, mw_h, mw)
        load(6, filt_h, filt)
        load(4, ib_h, ib)
        load(7, tab_h, tab)

        drain(x.at[0, 2 : 2 + WY, 0:WX], ld.at[1])
        drain(ipmt, ld.at[10])
        wv = x.at[me]

        def project_water(i, _):
            cells = wv[pl.ds(2 + 4 * i, 4), 0:WX, :].reshape(4 * WX, CO)
            got = dot_nt(ipmt[...], cells).astype(BF16)
            for j in range(4):
                ps[me, pl.ds((4 * i + j) * NF, NF), :] = got[:, j * WX : (j + 1) * WX]
            return 0

        lax.fori_loop(0, WY // 4, project_water, 0)
        pl.semaphore_wait(barrier, NC - 1 + NR - 1 + 9 + 4)
        for d in range(1, NR):
            pl.semaphore_signal(ready, inc=1, device_id=(me, rmod(row + d), col), device_id_type=MESH)

        send(ps.at[me], ps.at[me], csend.at[0], crecv.at[0], (other, row, col))

        def send_lat(t):
            pltpu.make_async_copy(atm.at[t * NC + col], g1.at[t, pl.ds(col * PM, PM)], g1r.at[t]).start()

            def step(p, _):
                there = shifted(p // NX, lax.rem(p, NX))
                send(
                    atm.at[t * NC + there], g1.at[t, pl.ds(col * PM, PM)], g1s.at[t], g1r.at[t], (me, row, there)
                )
                return 0

            lax.fori_loop(1, NC, step, 0)

        def water_sends(q):
            return [
                (row > 0, water.at[0:2], x.at[me, XR - 2 : XR, 0:WX], (q, rmod(row - 1), col)),
                (row < NR - 1, water.at[WY - 2 : WY], x.at[me, 0:2, 0:WX], (q, rmod(row + 1), col)),
                (col > 0, water.at[:, 0:16], hr.at[me, 2 : 2 + WY], (q, row, cmod(col - 1))),
                (col < NC - 1, water.at[:, WX - 16 : WX], hl.at[me, 2 : 2 + WY], (q, row, cmod(col + 1))),
                ((row > 0) & (col > 0), water.at[0:2, 0:16], hr.at[me, XR - 2 : XR],
                 (q, rmod(row - 1), cmod(col - 1))),
                ((row > 0) & (col < NC - 1), water.at[0:2, WX - 16 : WX], hl.at[me, XR - 2 : XR],
                 (q, rmod(row - 1), cmod(col + 1))),
                ((row < NR - 1) & (col > 0), water.at[WY - 2 : WY, 0:16], hr.at[me, 0:2],
                 (q, rmod(row + 1), cmod(col - 1))),
                ((row < NR - 1) & (col < NC - 1), water.at[WY - 2 : WY, WX - 16 : WX], hl.at[me, 0:2],
                 (q, rmod(row + 1), cmod(col + 1))),
            ]

        def water_recvs(q):
            return [
                (row < NR - 1, x.at[q, XR - 2 : XR, 0:WX]),
                (row > 0, x.at[q, 0:2, 0:WX]),
                (col < NC - 1, hr.at[q, 2 : 2 + WY]),
                (col > 0, hl.at[q, 2 : 2 + WY]),
                ((row < NR - 1) & (col < NC - 1), hr.at[q, XR - 2 : XR]),
                ((row < NR - 1) & (col > 0), hl.at[q, XR - 2 : XR]),
                ((row > 0) & (col < NC - 1), hr.at[q, 0:2]),
                ((row > 0) & (col > 0), hl.at[q, 0:2]),
            ]

        send_lat(0)

        def water_send(first, last):
            for q in range(2):
                for n, (there, src, dst, dev) in enumerate(water_sends(q)[first:last]):
                    @pl.when(there)
                    def _(src=src, dst=dst, dev=dev, n=n, q=q):
                        send(src, dst, wsend.at[first + n, q], wrecv.at[first + n, me], dev)

        water_send(0, 2)
        drain(atm_v, ld.at[0])
        drain(fwt, ld.at[11])

        def project_air(t, _):
            cells = atm_v[pl.ds(t * 4, 4)].reshape(4 * PM, C)
            got = dot_nt(fwt[...], cells)
            zeros = jnp.zeros((NF, 128 - PM), F32)
            for j in range(4):
                part = jnp.concatenate([got[:, j * PM : (j + 1) * PM], zeros], axis=1)
                pf[me, pl.ds((t * 4 + j) * NF, NF), :] = part.astype(BF16)
            return 0

        lax.fori_loop(0, PT // 4, project_air, 0)
        send(pf.at[me], pf.at[me], csend.at[1], crecv.at[1], (other, row, col))

        def both(part):
            return (part[0].astype(F32) + part[1].astype(F32)).astype(BF16)

        lane = lax.broadcasted_iota(jnp.int32, (16, 128), 1)
        line = lax.broadcasted_iota(jnp.int32, (16, 128), 0)

        def pick(cond):
            return jnp.where(cond, 1.0, 0.0).astype(BF16)

        def row_halo_send(tab_ref, rows, at):
            above = pl.ds((rows + 1) * NF, NF)
            below = pl.ds(rows * NF, NF)

            @pl.when(row > 0)
            def _():
                send(tab_ref.at[0:NF, 0:128], tab_ref.at[below, 0:128], hsend.at[at], hrecv.at[at],
                     (me, rmod(row - 1), col))

            @pl.when(row < NR - 1)
            def _():
                send(tab_ref.at[(rows - 1) * NF : rows * NF, 0:128], tab_ref.at[above, 0:128],
                     hsend.at[at + 1], hrecv.at[at + 1], (me, rmod(row + 1), col))

        def row_halo_recv(tab_ref, rows, at):
            above = pl.ds((rows + 1) * NF, NF)
            below = pl.ds(rows * NF, NF)

            @pl.when(row < NR - 1)
            def _():
                drain(tab_ref.at[below, 0:128], hrecv.at[at])

            @pl.when(row == NR - 1)
            def _():
                tab_ref[below, 0:128] = jnp.zeros((NF, 128), BF16)

            @pl.when(row > 0)
            def _():
                drain(tab_ref.at[above, 0:128], hrecv.at[at + 1])

            @pl.when(row == 0)
            def _():
                tab_ref[above, 0:128] = jnp.zeros((NF, 128), BF16)

        def sent(cond, ref, at):
            @pl.when(cond)
            def _():
                drain(ref, hsend.at[at])

        def row_halo_sent(tab_ref, at):
            sent(row > 0, tab_ref.at[0:NF, 0:128], at)
            sent(row < NR - 1, tab_ref.at[0:NF, 0:128], at + 1)

        def col_halo_send(tab_ref, edge, left, right, width, at):
            ends = pick(((line == 0) & (lane == 0)) | ((line == 1) & (lane == width - 1)))
            edge[...] = dot_nt(ends, tab_ref[:, 0:128]).astype(BF16)

            @pl.when(col > 0)
            def _():
                send(edge, right, hsend.at[at], hrecv.at[at], (me, row, cmod(col - 1)))

            @pl.when(col < NC - 1)
            def _():
                send(edge, left, hsend.at[at + 1], hrecv.at[at + 1], (me, row, cmod(col + 1)))

        def col_halo_recv(left, right, at):
            @pl.when(col < NC - 1)
            def _():
                drain(right, hrecv.at[at])

            @pl.when(col == NC - 1)
            def _():
                right[...] = jnp.zeros(right.shape, BF16)

            @pl.when(col > 0)
            def _():
                drain(left, hrecv.at[at + 1])

            @pl.when(col == 0)
            def _():
                left[...] = jnp.zeros(left.shape, BF16)

        def halo_columns(left, right, place):
            from_right = pick((line == 0) & (lane == place))
            from_left = pick((line == 1) & (lane == place + 1))
            return dot_tn(right[...], from_right) + dot_tn(left[...], from_left)

        def regrid(tab_ref, index, weight, rows, cols, block):
            cells = index.astype(F32)
            r_at = jnp.floor((cells + 0.5) * (1.0 / cols))
            c_at = cells - r_at * cols
            rsc[...] = jnp.where(r_at == 0, rows - 1.0, r_at - 1.0)
            csc[...] = jnp.where(c_at == 0, cols - 1.0, c_at - 1.0)
            wsc[...] = weight / jnp.sum(weight, axis=0, keepdims=True)
            width = tab_ref.shape[1]
            at = lax.broadcasted_iota(jnp.int32, (width, LANES), 0).astype(F32)

            def source(k, total):
                r_k = rsc[pl.ds(k, 1), :]
                c_k = csc[pl.ds(k, 1), :]
                w_k = wsc[pl.ds(k, 1), :]
                chosen = jnp.where(at == c_k, 1.0, 0.0).astype(BF16)
                for b in range(rows // block):
                    lines = dot(tab_ref[b * block * NF : (b + 1) * block * NF, :], chosen)
                    for j in range(block):
                        share = jnp.where(r_k == float(b * block + j), w_k, 0.0)
                        total = total + lines[j * NF : (j + 1) * NF] * share
                return total

            return lax.fori_loop(0, 4, source, jnp.zeros((NF, LANES), F32))

        drain(ps.at[0], crecv.at[0])
        ts[0 : WY * NF, 0:128] = both(ps)
        row_halo_send(ts, WY, 0)
        row_halo_recv(ts, WY, 0)
        col_halo_send(ts, es, esl, esr, WX, 4)
        send_lat(1)
        send(water, x.at[me, 2 : 2 + WY, 0:WX], wsend.at[8, 0], wrecv.at[8, 0], (other, row, col))

        drain(pf.at[0], crecv.at[1])
        tf[0 : PT * NF, :] = both(pf)
        row_halo_send(tf, PT, 2)

        col_halo_recv(esl, esr, 4)
        row_halo_sent(ts, 0)
        ts[:, 128:256] = halo_columns(esl, esr, 0).astype(BF16)

        for n, ref in ((12, aidx), (13, aw), (14, drv)):
            drain(ref, ld.at[n])

        def to_air(i, _):
            c = me * HC + i
            idx = jnp.concatenate(
                [aidx[t * NC + c] for t in range(LT)] + [jnp.zeros((4, LANES - LT * PM), jnp.int32)], axis=1
            )
            wgt = jnp.concatenate(
                [aw[t * NC + c] for t in range(LT)] + [jnp.ones((4, LANES - LT * PM), F32)], axis=1
            )
            ss[c] = regrid(ts, idx, wgt, OR, OC, 13 if OR % 13 == 0 else 1).astype(BF16)
            send(ss.at[c], sr.at[col], sss, ssr, (other, row, c))
            send(ss.at[c], ss.at[c], shs, shr, (other, row, col))

            @pl.when(c != col)
            def _():
                send(ss.at[c], sr.at[col], sss, ssr, (me, row, c))

            @pl.when(c == col)
            def _():
                pltpu.make_async_copy(ss.at[c], sr.at[col], ssr).start()

            return 0

        lax.fori_loop(0, HC, to_air, 0)
        send_lat(2)
        water_send(2, 8)

        drain(tabt, ld.at[2])
        drain(sr, ssr)

        def lift_terms(c, _):
            dsc[c] = dot_tn(sr[c], drv[...])
            return 0

        lax.fori_loop(0, NC, lift_terms, 0)

        pl.semaphore_wait(ready, NR - 1)

        for t in range(LT):
            drain(g1.at[t], g1r.at[t])

            def lift_lat(c, _, t=t):
                rows = pl.ds(pl.multiple_of(c * PM, PM), PM)
                g1[t, rows, :] = (
                    g1[t, rows, :].astype(F32) + dsc[c, t * PM : (t + 1) * PM, :]
                ).astype(BF16)
                return 0

            lax.fori_loop(0, NC, lift_lat, 0)

            def analyse(b, _, t=t):
                rows = pl.ds(pl.multiple_of(b * FB, FB), FB)
                got = dot(tabt[rows, :], g1[t])
                halves = [got[:, h * 128 : (h + 1) * 128].reshape(FB // 8, 8, 128) for h in range(2)]
                sp[t, pl.ds(b * (FB // 8), FB // 8)] = jnp.concatenate(halves, axis=1).astype(BF16)
                return 0

            lax.fori_loop(0, 4, analyse, 0)
            pltpu.make_async_copy(sp.at[t, flat], rx.at[t, flat], r2.at[t]).start()

            def scatter(p, _, t=t):
                r_to, c_to = partner(p)
                send(sp.at[t, r_to * NC + c_to], rx.at[t, flat], s2s.at[t], r2.at[t], (me, r_to, c_to))
                return 0

            lax.fori_loop(1, ND, scatter, 0)

        drain(ss.at[0:HC], shr)

        def lift_here(c, _):
            term = dot_tn(ss[c], drv[...])
            for t in range(LT):
                n = t * NC + c
                lf[n] = (atm_v[n].astype(F32) + term[t * PM : (t + 1) * PM]).astype(BF16)
            return 0

        lax.fori_loop(0, NC, lift_here, 0)
        pltpu.make_async_copy(lf, lifted_out, outs.at[1]).start()

        drain(fb, ld.at[3])
        lat_in = lax.broadcasted_iota(jnp.int32, (NLAT, NLAT), 0)
        lat_to = lax.broadcasted_iota(jnp.int32, (NLAT, NLAT), 1)
        t_to, d_to = lat_to // ND, lax.rem(lat_to, ND)
        order = pick(lat_in == (d_to // NC) * PT + t_to * NC + lax.rem(d_to, NC))

        def reorder(k, _):
            fbp[k] = dot(fb[k], order).astype(BF16)
            return 0

        lax.fori_loop(0, KB, reorder, 0)

        row_halo_recv(tf, PT, 2)
        col_halo_send(tf, ef, efl, efr, PM, 6)

        for q in range(2):
            for n, (there, dst) in enumerate(water_recvs(q)):
                @pl.when(there)
                def _(dst=dst, n=n, q=q):
                    drain(dst, wrecv.at[n, q])
        drain(x.at[0, 2 : 2 + WY, 0:WX], wrecv.at[8, 0])

        @pl.when(row == 0)
        def _():
            x[:, 0:2, 0:WX, :] = jnp.zeros((2, 2, WX, CO), BF16)

        @pl.when(row == NR - 1)
        def _():
            x[:, XR - 2 : XR, 0:WX, :] = jnp.zeros((2, 2, WX, CO), BF16)

        def side(i, _):
            inside = ((i >= 2) | (row > 0)) & ((i < XR - 2) | (row < NR - 1))
            sub = lax.broadcasted_iota(jnp.int32, (16, CO), 0)
            for q in range(2):
                from_right = jnp.where((sub < 2) & inside & (col < NC - 1), hr[q, i].astype(F32), 0.0)
                from_left = jnp.where((sub >= 14) & inside & (col > 0), hl[q, i].astype(F32), 0.0)
                x[q, i, WX:WP, :] = (from_right + from_left).astype(BF16)
            return 0

        lax.fori_loop(0, XR, side, 0)
        drain(w1, ld.at[8])

        def taps(src, weight, first, count):
            lhs = jnp.concatenate(
                [
                    jnp.concatenate([src[q, first + j + a] for a in range(3) for q in range(2)], axis=1)
                    for j in range(count)
                ],
                axis=0,
            )
            got = dot(lhs, weight[...])
            outs_ = []
            for j in range(count):
                part = got[j * WP : (j + 1) * WP]
                outs_.append(
                    pltpu.roll(part[:, 0:CO], 1, 0)
                    + part[:, CO : 2 * CO]
                    + pltpu.roll(part[:, 2 * CO : 3 * CO], WP - 1, 0)
                )
            return outs_

        def conv_first(i, _):
            place = lax.broadcasted_iota(jnp.int32, (WP, CO), 0)
            edge = ((place == WP - 1) & (col == 0)) | ((place == WX) & (col == NC - 1))
            for j, out in enumerate(taps(x, w1, 2 * i, 2)):
                h = 2 * i + j
                outside = ((h == 0) & (row == 0)) | ((h == HR_ - 1) & (row == NR - 1))
                hd[me, h] = jnp.where(edge | outside, 0.0, gelu(out)).astype(BF16)
            return 0

        lax.fori_loop(0, HR_ // 2, conv_first, 0)
        send(hd.at[me], hd.at[me], hds, hdr, (other, row, col))

        col_halo_recv(efl, efr, 6)
        row_halo_sent(tf, 2)
        tf[...] = (tf[...].astype(F32) + halo_columns(efl, efr, PM)).astype(BF16)

        for n, ref in ((15, mask), (16, oidx), (17, ow), (18, flw)):
            drain(ref, ld.at[n])

        def to_ocean(j, _):
            i = me * HO + j
            idx = jnp.concatenate([oidx[2 * i], oidx[2 * i + 1]], axis=1)
            wgt = jnp.concatenate([ow[2 * i], ow[2 * i + 1]], axis=1)
            fx[i] = regrid(tf, idx, wgt, AR, AC, 10 if AR % 10 == 0 else 1).astype(BF16)
            send(fx.at[i], fx.at[i], fxs, fxr, (other, row, col))
            return 0

        lax.fori_loop(0, HO, to_ocean, 0)

        TB = 32 if ND % 32 == 0 else 8

        def widen(t):
            drain(rx.at[t], r2.at[t])

            def step(i, _):
                rows = pl.ds(pl.multiple_of(i * TB, TB), TB)
                out_rows = pl.ds(pl.multiple_of((t * ND + i * TB) * 16, TB * 16), TB * 16)
                rxf[out_rows, :] = rx[t, rows].astype(F32).reshape(TB * 16, 128)
                return 0

            lax.fori_loop(0, ND // TB, step, 0)

        def spectra_of(k, first, last):
            count = (last - first) * ND
            return jnp.concatenate(
                [rxf[pl.ds(first * ND * 16 + k + 8 * h, count, stride=16), :] for h in range(2)], axis=1
            ).astype(BF16)

        for t in range(LT - 1):
            widen(t)
        SPLIT = (LT - 1) * ND

        def to_modes_first(k, _):
            acc[k] = dot(fbp[k, :, 0:SPLIT], spectra_of(k, 0, LT - 1))
            return 0

        lax.fori_loop(0, KB, to_modes_first, 0)
        drain(mw, ld.at[5])
        drain(filt, ld.at[6])
        drain(ib, ld.at[4])
        widen(LT - 1)

        def to_modes(k, _):
            md[k] = (acc[k] + dot(fbp[k, :, SPLIT:NLAT], spectra_of(k, LT - 1, LT))).astype(BF16)
            send(md.at[k], mp.at[k], mds.at[k], mdr.at[k], (other, row, col))
            return 0

        lax.fori_loop(0, KB, to_modes, 0)

        def mix_own(k, _):
            acc[k] = dot(md[k], mw[pl.ds(pl.multiple_of(me * C, C), C), :])
            return 0

        lax.fori_loop(0, KB, mix_own, 0)

        def mix(k, _):
            drain(mp.at[k], mdr.at[k])
            mixed = acc[k] + dot(mp[k], mw[pl.ds(pl.multiple_of(other * C, C), C), :])
            ms[k] = (mixed * filt[...]).astype(BF16)
            return 0

        lax.fori_loop(0, KB, mix, 0)

        for t in range(LT):
            def to_synth(k, _, t=t):
                basis = ib[k].reshape(NR, LT, NC, DEG)[:, t].reshape(ND, DEG)
                got = dot(basis, ms[k])
                for h in range(2):
                    qf[pl.ds(k + 8 * h, ND, stride=16), :] = got[:, h * 128 : (h + 1) * 128]
                return 0

            lax.fori_loop(0, KB, to_synth, 0)

            def narrow(i, _, t=t):
                rows = pl.ds(pl.multiple_of(i * TB, TB), TB)
                in_rows = pl.ds(pl.multiple_of(i * TB * 16, TB * 16), TB * 16)
                qb[t, rows] = qf[in_rows, :].reshape(TB, 16, 128).astype(BF16)
                return 0

            lax.fori_loop(0, ND // TB, narrow, 0)
            pltpu.make_async_copy(qb.at[t, flat], vx.at[t, flat], q_r.at[t]).start()

            def gather_back(p, _, t=t):
                r_to, c_to = partner(p)
                send(qb.at[t, r_to * NC + c_to], vx.at[t, flat], q_s.at[t], q_r.at[t], (me, r_to, c_to))
                return 0

            lax.fori_loop(1, ND, gather_back, 0)

        drain(hd.at[0], hdr)
        drain(fx.at[0:HO], fxr)
        drain(w2, ld.at[9])

        def conv_second(i, _):
            outs_ = taps(hd, w2, 2 * i, 2)
            sixteenth = jnp.full((NF, CO), 1.0 / NF, BF16)
            for j in range(2):
                r = 2 * i + j
                lift = dot_tn(fx[i, :, j * WX : (j + 1) * WX], flw[...])
                line_mask = jnp.broadcast_to(mask[pl.ds(r, 1), :].astype(F32), (NF, WX)).astype(BF16)
                keep = dot_tn(line_mask, sixteenth)
                here = x[me, r + 2, 0:WX, :].astype(F32)
                oo[r] = (here + keep * (outs_[j][0:WX] + lift)).astype(BF16)
            return 0

        lax.fori_loop(0, WY // 2, conv_second, 0)
        pltpu.make_async_copy(oo, ocean_out, outs.at[0]).start()

        drain(tab, ld.at[7])
        for t in range(LT):
            drain(vx.at[t], q_r.at[t])
            for h in range(2):
                part = vx[t].astype(F32)[:, 8 * h : 8 * h + 8, :].reshape(NLON, 128)
                bx[:, h * 128 : (h + 1) * 128] = part.astype(BF16)

            def synthesise(b, _, t=t):
                y = lax.rem(col // NX + b, NY)
                rows = pl.ds(pl.multiple_of(y * NX * PM, NX * PM), NX * PM)
                gs[t, rows, :] = dot(tab[rows, :], bx[...]).astype(BF16)

                def home(p, _):
                    there = y * NX + lax.rem(lax.rem(col, NX) + p, NX)

                    @pl.when(there != col)
                    def _():
                        send(gs.at[t, pl.ds(there * PM, PM)], grid_out.at[t * NC + col], gss.at[t], gsr.at[t],
                             (me, row, there))

                    @pl.when(there == col)
                    def _():
                        pltpu.make_async_copy(
                            gs.at[t, pl.ds(col * PM, PM)], grid_out.at[t * NC + col], gsr.at[t]
                        ).start()

                    return 0

                lax.fori_loop(0, NX, home, 0)
                return 0

            lax.fori_loop(0, NY, synthesise, 0)

        for t in range(LT):
            drain(grid_out.at[0:NC], gsr.at[t])

        for t in range(LT):
            drain(g1.at[t, 0 : (NC - 1) * PM], g1s.at[t])
            drain(sp.at[t, 0 : ND - 1], s2s.at[t])
            drain(vx.at[t, 0 : ND - 1], q_s.at[t])
            drain(gs.at[t, 0 : (NC - 1) * PM], gss.at[t])
        drain(sr.at[0 : NC - 1], sss)

        @pl.when((col < me * HC) | (col >= me * HC + HC))
        def _():
            drain(sr.at[0], sss)

        drain(ss.at[0:HC], shs)
        drain(fx.at[0:HO], fxs)
        for q in range(2):
            for n, (there, src, dst, dev) in enumerate(water_sends(q)):
                @pl.when(there)
                def _(src=src, n=n, q=q):
                    drain(src, wsend.at[n, q])
        drain(water, wsend.at[8, 0])
        drain(ps.at[0], csend.at[0])
        drain(pf.at[0], csend.at[1])
        drain(hd.at[0], hds)
        for k in range(KB):
            drain(mp.at[k], mds.at[k])
        for at, edge in ((4, es), (6, ef)):
            sent(col > 0, edge, at)
            sent(col < NC - 1, edge, at + 1)
        drain(oo, outs.at[0])
        drain(lf, outs.at[1])

    v = pltpu.VMEM
    dma = pltpu.SemaphoreType.DMA
    scratch = [
        v((WY, WX), jnp.int32), v((WY, 4, WX), jnp.int32), v((WY, 4, WX), F32), v((PT, 4, PM), jnp.int32),
        v((PT, 4, PM), F32), v((NF, C), BF16), v((NF, CO), BF16), v((NF, CO), BF16), v((NF, C), BF16),
        v((PT, PM, C), BF16), v((LT, NLON, C), BF16), v((NLON, NLON), BF16), v((NLON, NLON), BF16),
        v((LT, ND, 16, 128), BF16), v((LT, ND, 16, 128), BF16), v((NLAT * 16, 128), F32),
        v((KB, DEG, NLAT), BF16), v((KB, NLAT, DEG), BF16), v((KB, DEG, C), BF16), v((KB, DEG, C), BF16),
        v((2 * C, C), BF16), v((DEG, C), F32), v((ND * 16, 128), F32), v((LT, ND, 16, 128), BF16),
        v((LT, ND, 16, 128), BF16), v((NLON, C), BF16), v((LT, NLON, C), BF16), v((PT, PM, C), BF16),
        v((KB, DEG, NLAT), BF16), v((KB, DEG, C), F32), v((KB, DEG, C), BF16),
        v((2, XR, WP, CO), BF16), v((2, XR, 16, CO), BF16), v((2, XR, 16, CO), BF16), v((2, HR_, WP, CO), BF16),
        v((6 * CO, 3 * CO), BF16), v((6 * CO, 3 * CO), BF16), v((WY, WX, CO), BF16),
        v((NC, LANES, C), F32),
        v((AR * NF, 128), BF16), v((OR * NF, 256), BF16), v((2, PT * NF, 128), BF16), v((2, WY * NF, 128), BF16),
        v((16, AR * NF), BF16), v((16, OR * NF), BF16),
        v((16, AR * NF), BF16), v((16, AR * NF), BF16), v((16, OR * NF), BF16), v((16, OR * NF), BF16),
        v((4, LANES), F32), v((4, LANES), F32), v((4, LANES), F32),
        v((NC, NF, LANES), BF16), v((NC, NF, LANES), BF16), v((WY // 2, NF, LANES), BF16),
        dma((19,)), dma((9, 2)), dma((9, 2)), dma((2,)), dma((2,)), dma((8,)), dma((8,)),
        dma((LT,)), dma((LT,)), dma, dma, dma((LT,)), dma((LT,)), dma((KB,)), dma((KB,)),
        dma((LT,)), dma((LT,)), dma((LT,)), dma((LT,)), dma, dma, dma((2,)), dma, dma, dma, dma, pltpu.SemaphoreType.REGULAR,
    ]
    any_ = pl.BlockSpec(memory_space=pl.ANY)
    return pl.pallas_call(
        kernel,
        out_shape=(
            jax.ShapeDtypeStruct((PT, PM, C), BF16),
            jax.ShapeDtypeStruct((PT, PM, C), BF16),
            jax.ShapeDtypeStruct((WY, WX, CO), BF16),
        ),
        in_specs=[any_] * 19,
        out_specs=(any_, any_, any_),
        scratch_shapes=scratch,
        compiler_params=pltpu.CompilerParams(
            collective_id=0, has_side_effects=True, vmem_limit_bytes=60 * 1024 * 1024
        ),
        cost_estimate=pl.CostEstimate(flops=9_000_000_000, bytes_accessed=20_000_000, transcendentals=2_000_000),
        name="coupled_step",
    )


def solution(mesh):
    NR, NC = mesh.shape["row"], mesh.shape["col"]
    NX = 4 if NC == 16 else NC

    def local(
        atmosphere_state, water_condition, ocean_cell_mask, atmos_to_ocean_index, atmos_to_ocean_weight,
        water_source_positions, water_source_overlay_areas, flux_weight, flux_lift_weight,
        interface_projection_matrix, interface_driving_matrix, forward_basis, inverse_basis,
        mixing_weight, degree_filter, first_ocean_kernel, second_ocean_kernel,
    ):
        PT, PM, C = atmosphere_state.shape
        WY, WX, CO = water_condition.shape
        table = lon_table(NC * PM)
        step = make_kernel(
            NR, NC, NX, PT, PM, C, WY, WX, CO, flux_weight.shape[1], forward_basis.shape[1]
        )
        lifted, grid, ocean_out = step(
            atmosphere_state,
            water_condition,
            ocean_cell_mask,
            jnp.swapaxes(atmos_to_ocean_index, 1, 2),
            jnp.swapaxes(atmos_to_ocean_weight, 1, 2),
            jnp.swapaxes(water_source_positions, 1, 2),
            jnp.swapaxes(water_source_overlay_areas, 1, 2),
            flux_weight.T,
            flux_lift_weight,
            interface_projection_matrix.T,
            interface_driving_matrix,
            forward_basis,
            inverse_basis,
            mixing_weight,
            degree_filter,
            first_ocean_kernel,
            second_ocean_kernel,
            jnp.asarray(table),
            jnp.asarray(np.ascontiguousarray(table.T)),
        )
        atm_out = (lifted.astype(F32) + gelu(grid.astype(F32))).astype(BF16)
        return atm_out, ocean_out

    placed = (
        P("row", "col", "comp"),
        P("row", "col", "comp"),
        P("row", "col"),
        P("row", "col", None),
        P("row", "col", None),
        P("row", "col", None),
        P("row", "col", None),
        P("comp", None),
        P(None, "comp"),
        P("comp", None),
        P(None, "comp"),
        P(("row", "col"), None, None),
        P(("row", "col"), None, None),
        P(None, "comp"),
        P(None, "comp"),
        P(None, None, None, "comp"),
        P(None, None, None, "comp"),
    )
    return jax.shard_map(
        local,
        mesh=mesh,
        in_specs=placed,
        out_specs=(P("row", "col", "comp"), P("row", "col", "comp")),
        check_vma=False,
    )
```

```python
import math

import jax
import jax.numpy as jnp
import ml_dtypes
import numpy as np
from jax import lax
from jax.experimental import pallas as pl
from jax.experimental.pallas import tpu as pltpu
from jax.sharding import PartitionSpec as P

BF16 = jnp.bfloat16
F32 = jnp.float32
MESH = pl.DeviceIdType.MESH
LANES = 256


def lon_table(count):
    col_idx = np.arange(count, dtype=np.int64)[:, None]
    coef_idx = np.arange(count, dtype=np.int64)[None, :]
    half_count = count // 2
    freq = np.where(coef_idx <= half_count, coef_idx, coef_idx - half_count)
    phase = (col_idx * freq % count) * (2.0 * math.pi / count)
    values = np.where(coef_idx <= half_count, np.cos(phase), np.sin(phase))
    return (values * math.sqrt(2.0 / count)).astype(ml_dtypes.bfloat16)


def dot(a, b):
    return jnp.dot(a, b, preferred_element_type=F32)


def dot_nt(a, b):
    return lax.dot_general(a, b, (((1,), (1,)), ((), ())), preferred_element_type=F32)


def dot_tn(a, b):
    return lax.dot_general(a, b, (((0,), (0,)), ((), ())), preferred_element_type=F32)


def drain(ref, sem):
    pltpu.make_async_copy(ref, ref, sem).wait()


def gelu(x):
    return jax.nn.gelu(x, approximate=True)


def make_kernel(NR, NC, NX, PT, PM, C, WY, WX, CO, NF, DEG):
    LT = PT // NC
    NLON = NC * PM
    ND = NR * NC
    KB = NLON // ND
    NLAT = NR * PT
    NY = NC // NX
    HC, HO, W8 = NC // 2, WY // 4, WY // 8
    AR, AC = PT + 2, PM + 2
    OR, OC = WY + 2, WX + 2
    WP = WX + 16
    XR = WY + 4
    HR_ = WY + 2
    FB = NLON // 4

    def kernel(
        atm, water, mask_h, oidx_h, ow_h, aidx_h, aw_h, fwt_h, flw_h, ipmt_h, drv_h, fb_h, ib_h, mw_h, filt_h,
        k1_h, k2_h, tab_h, tabt_h, atm_out, ocean_out,
        mask, oidx, ow, aidx, aw, fwt, flw, ipmt, drv, ya, us, st, drv3, wl, wr,
        atm_v, g1, tabt, tab, sp, rx, rxf, fb, ib, md, mp, mw, filt, qf, qb, vx, bx, gs, hh, lf, fbp, acc, ms,
        x, hl, hr, hd, w1, w2, oo,
        tf, ts, pf, ps, ef, es, efl, efr, esl, esr, rsc, csc, wsc, ss, sr, fx,
        ld, wsend, wrecv, csend, crecv, hsend, hrecv, g1s, g1r, sss, ssr, s2s, r2, mds, mdr,
        q_s, q_r, gss, gsr, hds, hdr, outs, shs, shr, fxs, fxr, ready,
    ):
        me = lax.axis_index("comp")
        row = lax.axis_index("row")
        col = lax.axis_index("col")
        flat = row * NC + col
        other = 1 - me

        def rmod(v):
            return lax.rem(v + NR, NR)

        def cmod(v):
            return lax.rem(v + NC, NC)

        def shifted(py, px):
            y = lax.rem(col // NX + py, NY)
            xx = lax.rem(lax.rem(col, NX) + px, NX)
            return y * NX + xx

        def partner(p):
            return rmod(row + lax.rem(p, NR)), shifted(p // (NR * NX), lax.rem(p // NR, NX))

        def send(src, dst, ssem, rsem, dev):
            pltpu.make_async_remote_copy(
                src_ref=src, dst_ref=dst, send_sem=ssem, recv_sem=rsem, device_id=dev, device_id_type=MESH
            ).start()

        def load(i, src, dst):
            pltpu.make_async_copy(src, dst, ld.at[i]).start()

        barrier = pltpu.get_barrier_semaphore()

        def greet(dev):
            pl.semaphore_signal(barrier, inc=1, device_id=dev, device_id_type=MESH)

        for d in range(1, NC):
            greet((me, row, cmod(col + d)))
        for d in range(1, NR):
            greet((me, rmod(row + d), col))
        for dr in (-1, 0, 1):
            for dc in (-1, 0, 1):
                greet((other, rmod(row + dr), cmod(col + dc)))
                if dr and dc:
                    greet((me, rmod(row + dr), cmod(col + dc)))

        load(1, water, x.at[me, 2 : 2 + WY, 0:WX])
        load(10, ipmt_h, ipmt)
        load(0, atm, atm_v)
        for n, (src, dst) in enumerate(
            ((fwt_h, fwt), (aidx_h, aidx), (aw_h, aw), (drv_h, drv), (mask_h, mask), (oidx_h, oidx), (ow_h, ow),
             (flw_h, flw))
        ):
            load(11 + n, src, dst)
        load(2, tabt_h, tabt)
        load(3, fb_h, fb)
        for a in range(3):
            for b in range(3):
                rows = pl.ds(a * 2 * CO, 2 * CO)
                cols = pl.ds(b * CO, CO)
                pltpu.make_async_copy(k1_h.at[a, b], w1.at[rows, cols], ld.at[8]).start()
                pltpu.make_async_copy(k2_h.at[a, b], w2.at[rows, cols], ld.at[9]).start()
        load(5, mw_h, mw)
        load(6, filt_h, filt)
        load(4, ib_h, ib)
        load(7, tab_h, tab)

        drain(x.at[0, 2 : 2 + WY, 0:WX], ld.at[1])
        drain(ipmt, ld.at[10])
        wv = x.at[me]

        def project_water(i, _):
            cells = wv[pl.ds(2 + 4 * i, 4), 0:WX, :].reshape(4 * WX, CO)
            got = dot_nt(ipmt[...], cells).astype(BF16)
            for j in range(4):
                ps[me, pl.ds((4 * i + j) * NF, NF), :] = got[:, j * WX : (j + 1) * WX]
            return 0

        lax.fori_loop(0, WY // 4, project_water, 0)
        sub = lax.broadcasted_iota(jnp.int32, (16, CO), 0)

        def pack_edges(j, _):
            left = jnp.zeros((16, CO), F32)
            right = jnp.zeros((16, CO), F32)
            for m in range(8):
                mine = (sub >= 2 * m) & (sub < 2 * m + 2)
                head = x[me, 2 + 8 * j + m, 0:16, :].astype(F32)
                tail = x[me, 2 + 8 * j + m, WX - 16 : WX, :].astype(F32)
                left = jnp.where(mine, pltpu.roll(head, 2 * m, 0), left)
                right = jnp.where(mine, pltpu.roll(tail, (2 * m + 2) % 16, 0), right)
            wl[j] = left.astype(BF16)
            wr[j] = right.astype(BF16)
            return 0

        pl.semaphore_wait(barrier, NC - 1 + NR - 1 + 9 + 4)
        for d in range(1, NR):
            pl.semaphore_signal(ready, inc=1, device_id=(me, rmod(row + d), col), device_id_type=MESH)

        send(ps.at[me], ps.at[me], csend.at[0], crecv.at[0], (other, row, col))

        def send_lat(t):
            pltpu.make_async_copy(atm.at[t * NC + col], g1.at[t, pl.ds(col * PM, PM)], g1r.at[t]).start()

            def step(p, _):
                there = shifted(p // NX, lax.rem(p, NX))
                send(
                    atm.at[t * NC + there], g1.at[t, pl.ds(col * PM, PM)], g1s.at[t], g1r.at[t], (me, row, there)
                )
                return 0

            lax.fori_loop(1, NC, step, 0)

        def water_sends(q):
            return [
                (row > 0, water.at[0:2], x.at[me, XR - 2 : XR, 0:WX], (q, rmod(row - 1), col)),
                (row < NR - 1, water.at[WY - 2 : WY], x.at[me, 0:2, 0:WX], (q, rmod(row + 1), col)),
                (col > 0, wl, hr.at[me, 0:W8], (q, row, cmod(col - 1))),
                (col < NC - 1, wr, hl.at[me, 0:W8], (q, row, cmod(col + 1))),
                ((row > 0) & (col > 0), wl.at[0], hr.at[me, W8 + 1], (q, rmod(row - 1), cmod(col - 1))),
                ((row > 0) & (col < NC - 1), wr.at[0], hl.at[me, W8 + 1], (q, rmod(row - 1), cmod(col + 1))),
                ((row < NR - 1) & (col > 0), wl.at[W8 - 1], hr.at[me, W8], (q, rmod(row + 1), cmod(col - 1))),
                ((row < NR - 1) & (col < NC - 1), wr.at[W8 - 1], hl.at[me, W8],
                 (q, rmod(row + 1), cmod(col + 1))),
            ]

        def water_recvs(q):
            return [
                (row < NR - 1, x.at[q, XR - 2 : XR, 0:WX]),
                (row > 0, x.at[q, 0:2, 0:WX]),
                (col < NC - 1, hr.at[q, 0:W8]),
                (col > 0, hl.at[q, 0:W8]),
                ((row < NR - 1) & (col < NC - 1), hr.at[q, W8 + 1]),
                ((row < NR - 1) & (col > 0), hl.at[q, W8 + 1]),
                ((row > 0) & (col < NC - 1), hr.at[q, W8]),
                ((row > 0) & (col > 0), hl.at[q, W8]),
            ]

        send_lat(0)

        def water_send(first, last):
            for q in range(2):
                for n, (there, src, dst, dev) in enumerate(water_sends(q)[first:last]):
                    @pl.when(there)
                    def _(src=src, dst=dst, dev=dev, n=n, q=q):
                        send(src, dst, wsend.at[first + n, q], wrecv.at[first + n, me], dev)

        water_send(0, 2)

        def both(part):
            return (part[0].astype(F32) + part[1].astype(F32)).astype(BF16)

        lane = lax.broadcasted_iota(jnp.int32, (16, 128), 1)
        line = lax.broadcasted_iota(jnp.int32, (16, 128), 0)

        def pick(cond):
            return jnp.where(cond, 1.0, 0.0).astype(BF16)

        def halo_parts(tab_ref, edge, left, right, rows):
            above = pl.ds((rows + 1) * NF, NF)
            below = pl.ds(rows * NF, NF)
            parts = [
                (row > 0, row < NR - 1, tab_ref.at[0:NF, 0:128], tab_ref.at[below, 0:128], (-1, 0)),
                (row < NR - 1, row > 0, tab_ref.at[(rows - 1) * NF : rows * NF, 0:128], tab_ref.at[above, 0:128],
                 (1, 0)),
            ]
            for dr in (-1, 0, 1):
                to = (row > 0) if dr < 0 else (row < NR - 1) if dr > 0 else (row >= 0)
                fro = (row < NR - 1) if dr < 0 else (row > 0) if dr > 0 else (row >= 0)
                parts.append((to & (col > 0), fro & (col < NC - 1), edge, right.at[1 - dr], (dr, -1)))
                parts.append((to & (col < NC - 1), fro & (col > 0), edge, left.at[1 - dr], (dr, 1)))
            return parts

        def halo_send(tab_ref, edge, left, right, rows, width, at):
            ends = pick(((line == 0) & (lane == 0)) | ((line == 1) & (lane == width - 1)))
            edge[...] = dot_nt(ends, tab_ref[0 : rows * NF, 0:128]).astype(BF16)
            for n, (to, _, src, dst, (dr, dc)) in enumerate(halo_parts(tab_ref, edge, left, right, rows)):
                @pl.when(to)
                def _(src=src, dst=dst, n=n, dr=dr, dc=dc):
                    send(src, dst, hsend.at[at + n], hrecv.at[at + n], (me, rmod(row + dr), cmod(col + dc)))

        def halo_recv(tab_ref, edge, left, right, rows, at):
            for n, (_, fro, src, dst, _) in enumerate(halo_parts(tab_ref, edge, left, right, rows)):
                @pl.when(fro)
                def _(dst=dst, n=n):
                    drain(dst, hrecv.at[at + n])

            @pl.when(row == NR - 1)
            def _():
                tab_ref[rows * NF : (rows + 1) * NF, 0:128] = jnp.zeros((NF, 128), BF16)

            @pl.when(row == 0)
            def _():
                tab_ref[(rows + 1) * NF : (rows + 2) * NF, 0:128] = jnp.zeros((NF, 128), BF16)

        def halo_sent(tab_ref, edge, left, right, rows, at, first, last):
            for n, (to, _, src, _, _) in enumerate(halo_parts(tab_ref, edge, left, right, rows)):
                if first <= n < last:
                    @pl.when(to)
                    def _(src=src, n=n):
                        drain(src, hsend.at[at + n])

        def halo_columns(left, right, rows, place):
            def column(got, inside):
                mid = jnp.where(inside, got[1].astype(F32), 0.0)
                below = jnp.where(inside & (row < NR - 1), got[2].astype(F32)[:, 0:NF], 0.0)
                above = jnp.where(inside & (row > 0), got[0].astype(F32)[:, (rows - 1) * NF : rows * NF], 0.0)
                return jnp.concatenate([mid, below, above], axis=1).astype(BF16)

            from_right = pick((line == 0) & (lane == place))
            from_left = pick((line == 1) & (lane == place + 1))
            return dot_tn(column(right, col < NC - 1), from_right) + dot_tn(column(left, col > 0), from_left)

        def regrid(tab_ref, index, weight, rows, cols, block):
            cells = index.astype(F32)
            r_at = jnp.floor((cells + 0.5) * (1.0 / cols))
            c_at = cells - r_at * cols
            rsc[...] = jnp.where(r_at == 0, rows - 1.0, r_at - 1.0)
            csc[...] = jnp.where(c_at == 0, cols - 1.0, c_at - 1.0)
            wsc[...] = weight / jnp.sum(weight, axis=0, keepdims=True)
            width = tab_ref.shape[1]
            at = lax.broadcasted_iota(jnp.int32, (width, LANES), 0).astype(F32)

            def source(k, total):
                r_k = rsc[pl.ds(k, 1), :]
                c_k = csc[pl.ds(k, 1), :]
                w_k = wsc[pl.ds(k, 1), :]
                chosen = jnp.where(at == c_k, 1.0, 0.0).astype(BF16)
                for b in range(rows // block):
                    lines = dot(tab_ref[b * block * NF : (b + 1) * block * NF, :], chosen)
                    for j in range(block):
                        share = jnp.where(r_k == float(b * block + j), w_k, 0.0)
                        total = total + lines[j * NF : (j + 1) * NF] * share
                return total

            return lax.fori_loop(0, 4, source, jnp.zeros((NF, LANES), F32))

        drain(ps.at[0], crecv.at[0])
        ts[0 : WY * NF, 0:128] = both(ps)
        halo_send(ts, es, esl, esr, WY, WX, 0)

        drain(atm_v, ld.at[0])
        drain(fwt, ld.at[11])

        def project_air(t, _):
            cells = atm_v[pl.ds(t * 4, 4)].reshape(4 * PM, C)
            got = dot_nt(fwt[...], cells)
            zeros = jnp.zeros((NF, 128 - PM), F32)
            for j in range(4):
                part = jnp.concatenate([got[:, j * PM : (j + 1) * PM], zeros], axis=1)
                pf[me, pl.ds((t * 4 + j) * NF, NF), :] = part.astype(BF16)
            return 0

        lax.fori_loop(0, PT // 4, project_air, 0)
        send(pf.at[me], pf.at[me], csend.at[1], crecv.at[1], (other, row, col))

        send_lat(1)
        halo_recv(ts, es, esl, esr, WY, 0)
        halo_sent(ts, es, esl, esr, WY, 0, 0, 2)
        ts[:, 128:256] = halo_columns(esl, esr, WY, 0).astype(BF16)

        for n, ref in ((12, aidx), (13, aw), (14, drv)):
            drain(ref, ld.at[n])

        def to_air(i, _):
            c = me * HC + i
            idx = jnp.concatenate(
                [aidx[t * NC + c] for t in range(LT)] + [jnp.zeros((4, LANES - LT * PM), jnp.int32)], axis=1
            )
            wgt = jnp.concatenate(
                [aw[t * NC + c] for t in range(LT)] + [jnp.ones((4, LANES - LT * PM), F32)], axis=1
            )
            ss[c] = regrid(ts, idx, wgt, OR, OC, 13 if OR % 13 == 0 else 1).astype(BF16)
            send(ss.at[c], sr.at[col], sss, ssr, (other, row, c))
            send(ss.at[c], ss.at[c], shs, shr, (other, row, col))

            @pl.when(c != col)
            def _():
                send(ss.at[c], sr.at[col], sss, ssr, (me, row, c))

            @pl.when(c == col)
            def _():
                pltpu.make_async_copy(ss.at[c], sr.at[col], ssr).start()

            return 0

        lax.fori_loop(0, HC, to_air, 0)
        send_lat(2)
        lax.fori_loop(0, W8, pack_edges, 0)
        water_send(2, 8)
        send(water, x.at[me, 2 : 2 + WY, 0:WX], wsend.at[8, 0], wrecv.at[8, 0], (other, row, col))
        drain(pf.at[0], crecv.at[1])
        tf[0 : PT * NF, :] = both(pf)
        halo_send(tf, ef, efl, efr, PT, PM, 8)

        drain(tabt, ld.at[2])

        for t in range(LT):
            drain(g1.at[t], g1r.at[t])

            def analyse(b, _, t=t):
                rows = pl.ds(pl.multiple_of(b * FB, FB), FB)
                ya[t, rows, :] = dot(tabt[rows, :], g1[t])
                return 0

            lax.fori_loop(0, 4, analyse, 0)

        drv3[...] = jnp.zeros(drv3.shape, BF16)
        for t in range(LT):
            drv3[t, t * NF : (t + 1) * NF, :] = drv[...]
        drain(sr, ssr)
        for t in range(LT):
            st[t * NF : (t + 1) * NF, :] = jnp.concatenate(
                [sr[c].astype(F32)[:, t * PM : (t + 1) * PM] for c in range(NC)], axis=1
            ).astype(BF16)

        def analyse_fields(b, _):
            rows = pl.ds(pl.multiple_of(b * FB, FB), FB)
            us[rows, :] = dot_nt(tabt[rows, :], st[...]).astype(BF16)
            return 0

        lax.fori_loop(0, 4, analyse_fields, 0)
        pl.semaphore_wait(ready, NR - 1)

        for t in range(LT):
            def force(b, _, t=t):
                rows = pl.ds(pl.multiple_of(b * FB, FB), FB)
                got = ya[t, rows, :] + dot(us[rows, :], drv3[t])
                halves = [got[:, h * 128 : (h + 1) * 128].reshape(FB // 8, 8, 128) for h in range(2)]
                sp[t, pl.ds(b * (FB // 8), FB // 8)] = jnp.concatenate(halves, axis=1).astype(BF16)
                return 0

            lax.fori_loop(0, 4, force, 0)
            pltpu.make_async_copy(sp.at[t, flat], rx.at[t, flat], r2.at[t]).start()

            def scatter(p, _, t=t):
                r_to, c_to = partner(p)
                send(sp.at[t, r_to * NC + c_to], rx.at[t, flat], s2s.at[t], r2.at[t], (me, r_to, c_to))
                return 0

            lax.fori_loop(1, ND, scatter, 0)

        drain(ss.at[0:HC], shr)

        def lift_here(c, _):
            term = dot_tn(ss[c], drv[...])
            for t in range(LT):
                n = t * NC + c
                lf[n] = (atm_v[n].astype(F32) + term[t * PM : (t + 1) * PM]).astype(BF16)
            return 0

        lax.fori_loop(0, NC, lift_here, 0)

        drain(fb, ld.at[3])
        lat_in = lax.broadcasted_iota(jnp.int32, (NLAT, NLAT), 0)
        lat_to = lax.broadcasted_iota(jnp.int32, (NLAT, NLAT), 1)
        t_to, d_to = lat_to // ND, lax.rem(lat_to, ND)
        order = pick(lat_in == (d_to // NC) * PT + t_to * NC + lax.rem(d_to, NC))

        def reorder(k, _):
            fbp[k] = dot(fb[k], order).astype(BF16)
            return 0

        lax.fori_loop(0, KB, reorder, 0)

        for q in range(2):
            for n, (there, dst) in enumerate(water_recvs(q)):
                @pl.when(there)
                def _(dst=dst, n=n, q=q):
                    drain(dst, wrecv.at[n, q])
        drain(x.at[0, 2 : 2 + WY, 0:WX], wrecv.at[8, 0])

        @pl.when(row == 0)
        def _():
            x[:, 0:2, 0:WX, :] = jnp.zeros((2, 2, WX, CO), BF16)

        @pl.when(row == NR - 1)
        def _():
            x[:, XR - 2 : XR, 0:WX, :] = jnp.zeros((2, 2, WX, CO), BF16)

        def side(i, tile, m, inside):
            for q in range(2):
                from_right = pltpu.roll(hr[q, tile].astype(F32), (16 - 2 * m) % 16, 0)
                from_left = pltpu.roll(hl[q, tile].astype(F32), (30 - 2 * m) % 16, 0)
                cells = jnp.where(
                    (sub < 2) & inside & (col < NC - 1),
                    from_right,
                    jnp.where((sub >= 14) & inside & (col > 0), from_left, 0.0),
                )
                x[q, i, WX:WP, :] = cells.astype(BF16)

        def sides(j, _):
            for m in range(8):
                side(2 + 8 * j + m, j, m, True)
            return 0

        lax.fori_loop(0, W8, sides, 0)
        for m in range(2):
            side(m, W8, 6 + m, row > 0)
            side(XR - 2 + m, W8 + 1, m, row < NR - 1)
        drain(w1, ld.at[8])

        def taps(src, weight, first, count):
            lhs = jnp.concatenate(
                [
                    jnp.concatenate([src[q, first + j + a] for a in range(3) for q in range(2)], axis=1)
                    for j in range(count)
                ],
                axis=0,
            )
            got = dot(lhs, weight[...])
            outs_ = []
            for j in range(count):
                part = got[j * WP : (j + 1) * WP]
                outs_.append(
                    pltpu.roll(part[:, 0:CO], 1, 0)
                    + part[:, CO : 2 * CO]
                    + pltpu.roll(part[:, 2 * CO : 3 * CO], WP - 1, 0)
                )
            return outs_

        def conv_first(i, _):
            place = lax.broadcasted_iota(jnp.int32, (WP, CO), 0)
            edge = ((place == WP - 1) & (col == 0)) | ((place == WX) & (col == NC - 1))
            for j, out in enumerate(taps(x, w1, 2 * i, 2)):
                h = 2 * i + j
                outside = ((h == 0) & (row == 0)) | ((h == HR_ - 1) & (row == NR - 1))
                hd[me, h] = jnp.where(edge | outside, 0.0, gelu(out)).astype(BF16)
            return 0

        lax.fori_loop(0, HR_ // 2, conv_first, 0)
        send(hd.at[me], hd.at[me], hds, hdr, (other, row, col))

        halo_recv(tf, ef, efl, efr, PT, 8)
        halo_sent(tf, ef, efl, efr, PT, 8, 0, 2)
        tf[...] = (tf[...].astype(F32) + halo_columns(efl, efr, PT, PM)).astype(BF16)

        for n, ref in ((15, mask), (16, oidx), (17, ow), (18, flw)):
            drain(ref, ld.at[n])

        def to_ocean(j, _):
            i = me * HO + j
            idx = jnp.concatenate([oidx[2 * i], oidx[2 * i + 1]], axis=1)
            wgt = jnp.concatenate([ow[2 * i], ow[2 * i + 1]], axis=1)
            fx[i] = regrid(tf, idx, wgt, AR, AC, 10 if AR % 10 == 0 else 1).astype(BF16)
            send(fx.at[i], fx.at[i], fxs, fxr, (other, row, col))
            return 0

        lax.fori_loop(0, HO, to_ocean, 0)

        TB = 32 if ND % 32 == 0 else 8

        def widen(t):
            drain(rx.at[t], r2.at[t])

            def step(i, _):
                rows = pl.ds(pl.multiple_of(i * TB, TB), TB)
                out_rows = pl.ds(pl.multiple_of((t * ND + i * TB) * 16, TB * 16), TB * 16)
                rxf[out_rows, :] = rx[t, rows].astype(F32).reshape(TB * 16, 128)
                return 0

            lax.fori_loop(0, ND // TB, step, 0)

        def spectra_of(k, first, last):
            count = (last - first) * ND
            return jnp.concatenate(
                [rxf[pl.ds(first * ND * 16 + k + 8 * h, count, stride=16), :] for h in range(2)], axis=1
            ).astype(BF16)

        for t in range(LT - 1):
            widen(t)
        SPLIT = (LT - 1) * ND

        def to_modes_first(k, _):
            acc[k] = dot(fbp[k, :, 0:SPLIT], spectra_of(k, 0, LT - 1))
            return 0

        lax.fori_loop(0, KB, to_modes_first, 0)
        drain(mw, ld.at[5])
        drain(filt, ld.at[6])
        drain(ib, ld.at[4])
        widen(LT - 1)

        def to_modes(k, _):
            md[k] = (acc[k] + dot(fbp[k, :, SPLIT:NLAT], spectra_of(k, LT - 1, LT))).astype(BF16)
            send(md.at[k], mp.at[k], mds.at[k], mdr.at[k], (other, row, col))
            return 0

        lax.fori_loop(0, KB, to_modes, 0)

        def mix_own(k, _):
            acc[k] = dot(md[k], mw[pl.ds(pl.multiple_of(me * C, C), C), :])
            return 0

        lax.fori_loop(0, KB, mix_own, 0)

        def mix(k, _):
            drain(mp.at[k], mdr.at[k])
            mixed = acc[k] + dot(mp[k], mw[pl.ds(pl.multiple_of(other * C, C), C), :])
            ms[k] = (mixed * filt[...]).astype(BF16)
            return 0

        lax.fori_loop(0, KB, mix, 0)

        for t in range(LT):
            def to_synth(k, _, t=t):
                basis = ib[k].reshape(NR, LT, NC, DEG)[:, t].reshape(ND, DEG)
                got = dot(basis, ms[k])
                for h in range(2):
                    qf[pl.ds(k + 8 * h, ND, stride=16), :] = got[:, h * 128 : (h + 1) * 128]
                return 0

            lax.fori_loop(0, KB, to_synth, 0)

            def narrow(i, _, t=t):
                rows = pl.ds(pl.multiple_of(i * TB, TB), TB)
                in_rows = pl.ds(pl.multiple_of(i * TB * 16, TB * 16), TB * 16)
                qb[t, rows] = qf[in_rows, :].reshape(TB, 16, 128).astype(BF16)
                return 0

            lax.fori_loop(0, ND // TB, narrow, 0)
            pltpu.make_async_copy(qb.at[t, flat], vx.at[t, flat], q_r.at[t]).start()

            def gather_back(p, _, t=t):
                r_to, c_to = partner(p)
                send(qb.at[t, r_to * NC + c_to], vx.at[t, flat], q_s.at[t], q_r.at[t], (me, r_to, c_to))
                return 0

            lax.fori_loop(1, ND, gather_back, 0)

        drain(hd.at[0], hdr)
        drain(fx.at[0:HO], fxr)
        drain(w2, ld.at[9])

        def conv_second(i, _):
            outs_ = taps(hd, w2, 2 * i, 2)
            sixteenth = jnp.full((NF, CO), 1.0 / NF, BF16)
            for j in range(2):
                r = 2 * i + j
                lift = dot_tn(fx[i, :, j * WX : (j + 1) * WX], flw[...])
                line_mask = jnp.broadcast_to(mask[pl.ds(r, 1), :].astype(F32), (NF, WX)).astype(BF16)
                keep = dot_tn(line_mask, sixteenth)
                here = x[me, r + 2, 0:WX, :].astype(F32)
                oo[r] = (here + keep * (outs_[j][0:WX] + lift)).astype(BF16)
            return 0

        lax.fori_loop(0, WY // 2, conv_second, 0)
        pltpu.make_async_copy(oo, ocean_out, outs.at[0]).start()

        drain(tab, ld.at[7])
        for t in range(LT):
            drain(vx.at[t], q_r.at[t])
            for h in range(2):
                part = vx[t].astype(F32)[:, 8 * h : 8 * h + 8, :].reshape(NLON, 128)
                bx[:, h * 128 : (h + 1) * 128] = part.astype(BF16)

            def synthesise(b, _, t=t):
                y = lax.rem(col // NX + b, NY)
                rows = pl.ds(pl.multiple_of(y * NX * PM, NX * PM), NX * PM)
                gs[t, rows, :] = dot(tab[rows, :], bx[...]).astype(BF16)

                def home(p, _):
                    there = y * NX + lax.rem(lax.rem(col, NX) + p, NX)

                    @pl.when(there != col)
                    def _():
                        send(gs.at[t, pl.ds(there * PM, PM)], hh.at[t * NC + col], gss.at[t], gsr.at[t],
                             (me, row, there))

                    @pl.when(there == col)
                    def _():
                        pltpu.make_async_copy(
                            gs.at[t, pl.ds(col * PM, PM)], hh.at[t * NC + col], gsr.at[t]
                        ).start()

                    return 0

                lax.fori_loop(0, NX, home, 0)
                return 0

            lax.fori_loop(0, NY, synthesise, 0)

        for t in range(LT):
            drain(hh.at[t * NC : (t + 1) * NC], gsr.at[t])

            def finish(c, _, t=t):
                n = t * NC + c
                lf[n] = (lf[n].astype(F32) + gelu(hh[n].astype(F32))).astype(BF16)
                return 0

            lax.fori_loop(0, NC, finish, 0)
            done = pl.ds(t * NC, NC)
            pltpu.make_async_copy(lf.at[done], atm_out.at[done], outs.at[1]).start()

        for t in range(LT):
            drain(g1.at[t, 0 : (NC - 1) * PM], g1s.at[t])
            drain(sp.at[t, 0 : ND - 1], s2s.at[t])
            drain(vx.at[t, 0 : ND - 1], q_s.at[t])
            drain(gs.at[t, 0 : (NC - 1) * PM], gss.at[t])
        drain(sr.at[0 : NC - 1], sss)

        @pl.when((col < me * HC) | (col >= me * HC + HC))
        def _():
            drain(sr.at[0], sss)

        drain(ss.at[0:HC], shs)
        drain(fx.at[0:HO], fxs)
        for q in range(2):
            for n, (there, src, dst, dev) in enumerate(water_sends(q)):
                @pl.when(there)
                def _(src=src, n=n, q=q):
                    drain(src, wsend.at[n, q])
        drain(water, wsend.at[8, 0])
        drain(ps.at[0], csend.at[0])
        drain(pf.at[0], csend.at[1])
        drain(hd.at[0], hds)
        for k in range(KB):
            drain(mp.at[k], mds.at[k])
        halo_sent(ts, es, esl, esr, WY, 0, 2, 8)
        halo_sent(tf, ef, efl, efr, PT, 8, 2, 8)
        drain(oo, outs.at[0])
        drain(lf, outs.at[1])

    v = pltpu.VMEM
    dma = pltpu.SemaphoreType.DMA
    scratch = [
        v((WY, WX), jnp.int32), v((WY, 4, WX), jnp.int32), v((WY, 4, WX), F32), v((PT, 4, PM), jnp.int32),
        v((PT, 4, PM), F32), v((NF, C), BF16), v((NF, CO), BF16), v((NF, CO), BF16), v((NF, C), BF16),
        v((LT, NLON, C), F32), v((NLON, LT * NF), BF16), v((LT * NF, NLON), BF16), v((LT, LT * NF, C), BF16),
        v((W8, 16, CO), BF16), v((W8, 16, CO), BF16),
        v((PT, PM, C), BF16), v((LT, NLON, C), BF16), v((NLON, NLON), BF16), v((NLON, NLON), BF16),
        v((LT, ND, 16, 128), BF16), v((LT, ND, 16, 128), BF16), v((NLAT * 16, 128), F32),
        v((KB, DEG, NLAT), BF16), v((KB, NLAT, DEG), BF16), v((KB, DEG, C), BF16), v((KB, DEG, C), BF16),
        v((2 * C, C), BF16), v((DEG, C), F32), v((ND * 16, 128), F32), v((LT, ND, 16, 128), BF16),
        v((LT, ND, 16, 128), BF16), v((NLON, C), BF16), v((LT, NLON, C), BF16), v((PT, PM, C), BF16), v((PT, PM, C), BF16),
        v((KB, DEG, NLAT), BF16), v((KB, DEG, C), F32), v((KB, DEG, C), BF16),
        v((2, XR, WP, CO), BF16), v((2, W8 + 2, 16, CO), BF16), v((2, W8 + 2, 16, CO), BF16), v((2, HR_, WP, CO), BF16),
        v((6 * CO, 3 * CO), BF16), v((6 * CO, 3 * CO), BF16), v((WY, WX, CO), BF16),
        v((AR * NF, 128), BF16), v((OR * NF, 256), BF16), v((2, PT * NF, 128), BF16), v((2, WY * NF, 128), BF16),
        v((16, PT * NF), BF16), v((16, WY * NF), BF16),
        v((3, 16, PT * NF), BF16), v((3, 16, PT * NF), BF16), v((3, 16, WY * NF), BF16), v((3, 16, WY * NF), BF16),
        v((4, LANES), F32), v((4, LANES), F32), v((4, LANES), F32),
        v((NC, NF, LANES), BF16), v((NC, NF, LANES), BF16), v((WY // 2, NF, LANES), BF16),
        dma((19,)), dma((9, 2)), dma((9, 2)), dma((2,)), dma((2,)), dma((16,)), dma((16,)),
        dma((LT,)), dma((LT,)), dma, dma, dma((LT,)), dma((LT,)), dma((KB,)), dma((KB,)),
        dma((LT,)), dma((LT,)), dma((LT,)), dma((LT,)), dma, dma, dma((2,)), dma, dma, dma, dma, pltpu.SemaphoreType.REGULAR,
    ]
    any_ = pl.BlockSpec(memory_space=pl.ANY)
    return pl.pallas_call(
        kernel,
        out_shape=(
            jax.ShapeDtypeStruct((PT, PM, C), BF16),
            jax.ShapeDtypeStruct((WY, WX, CO), BF16),
        ),
        in_specs=[any_] * 19,
        out_specs=(any_, any_),
        scratch_shapes=scratch,
        compiler_params=pltpu.CompilerParams(
            collective_id=0, has_side_effects=True, vmem_limit_bytes=60 * 1024 * 1024
        ),
        cost_estimate=pl.CostEstimate(flops=9_000_000_000, bytes_accessed=20_000_000, transcendentals=2_000_000),
        name="coupled_step",
    )


def settle(*arrays):
    pieces = 8 if all(a.shape[0] % 8 == 0 for a in arrays) else 4

    def kernel(*refs):
        count = len(arrays)
        sems = refs[-1]
        copies = []
        for n in range(count):
            step = arrays[n].shape[0] // pieces
            for p in range(pieces):
                part = pl.ds(p * step, step)
                copies.append(
                    pltpu.make_async_copy(refs[n].at[part], refs[count + n].at[part], sems.at[n, p])
                )
        for copy in copies:
            copy.start()
        for copy in copies:
            copy.wait()

    any_ = pl.BlockSpec(memory_space=pl.ANY)
    return pl.pallas_call(
        kernel,
        out_shape=tuple(jax.ShapeDtypeStruct(a.shape, a.dtype) for a in arrays),
        in_specs=[any_] * len(arrays),
        out_specs=tuple([any_] * len(arrays)),
        scratch_shapes=[pltpu.SemaphoreType.DMA((len(arrays), pieces))],
        name="settle",
    )(*arrays)


def solution(mesh):
    NR, NC = mesh.shape["row"], mesh.shape["col"]
    NX = 4 if NC == 16 else NC

    def local(
        atmosphere_state, water_condition, ocean_cell_mask, atmos_to_ocean_index, atmos_to_ocean_weight,
        water_source_positions, water_source_overlay_areas, flux_weight, flux_lift_weight,
        interface_projection_matrix, interface_driving_matrix, forward_basis, inverse_basis,
        mixing_weight, degree_filter, first_ocean_kernel, second_ocean_kernel,
    ):
        PT, PM, C = atmosphere_state.shape
        WY, WX, CO = water_condition.shape
        table = lon_table(NC * PM)
        step = make_kernel(
            NR, NC, NX, PT, PM, C, WY, WX, CO, flux_weight.shape[1], forward_basis.shape[1]
        )
        return settle(*step(
            atmosphere_state,
            water_condition,
            ocean_cell_mask,
            jnp.swapaxes(atmos_to_ocean_index, 1, 2),
            jnp.swapaxes(atmos_to_ocean_weight, 1, 2),
            jnp.swapaxes(water_source_positions, 1, 2),
            jnp.swapaxes(water_source_overlay_areas, 1, 2),
            flux_weight.T,
            flux_lift_weight,
            interface_projection_matrix.T,
            interface_driving_matrix,
            forward_basis,
            inverse_basis,
            mixing_weight,
            degree_filter,
            first_ocean_kernel,
            second_ocean_kernel,
            jnp.asarray(table),
            jnp.asarray(np.ascontiguousarray(table.T)),
        ))

    placed = (
        P("row", "col", "comp"),
        P("row", "col", "comp"),
        P("row", "col"),
        P("row", "col", None),
        P("row", "col", None),
        P("row", "col", None),
        P("row", "col", None),
        P("comp", None),
        P(None, "comp"),
        P("comp", None),
        P(None, "comp"),
        P(("row", "col"), None, None),
        P(("row", "col"), None, None),
        P(None, "comp"),
        P(None, "comp"),
        P(None, None, None, "comp"),
        P(None, None, None, "comp"),
    )
    return jax.shard_map(
        local,
        mesh=mesh,
        in_specs=placed,
        out_specs=(P("row", "col", "comp"), P("row", "col", "comp")),
        check_vma=False,
    )
```

```python
import math

import jax
import jax.numpy as jnp
import ml_dtypes
import numpy as np
from jax import lax
from jax.experimental import pallas as pl
from jax.experimental.pallas import tpu as pltpu
from jax.sharding import PartitionSpec as P

BF16 = jnp.bfloat16
F32 = jnp.float32
MESH = pl.DeviceIdType.MESH
LANES = 256


def lon_table(count):
    col_idx = np.arange(count, dtype=np.int64)[:, None]
    coef_idx = np.arange(count, dtype=np.int64)[None, :]
    half_count = count // 2
    freq = np.where(coef_idx <= half_count, coef_idx, coef_idx - half_count)
    phase = (col_idx * freq % count) * (2.0 * math.pi / count)
    values = np.where(coef_idx <= half_count, np.cos(phase), np.sin(phase))
    return (values * math.sqrt(2.0 / count)).astype(ml_dtypes.bfloat16)


def dot(a, b):
    return jnp.dot(a, b, preferred_element_type=F32)


def dot_nt(a, b):
    return lax.dot_general(a, b, (((1,), (1,)), ((), ())), preferred_element_type=F32)


def dot_tn(a, b):
    return lax.dot_general(a, b, (((0,), (0,)), ((), ())), preferred_element_type=F32)


def drain(ref, sem):
    pltpu.make_async_copy(ref, ref, sem).wait()


def gelu(x):
    return jax.nn.gelu(x, approximate=True)


def make_kernel(NR, NC, NX, PT, PM, C, WY, WX, CO, NF, DEG):
    LT = PT // NC
    NLON = NC * PM
    ND = NR * NC
    KB = NLON // ND
    NLAT = NR * PT
    NY = NC // NX
    HC, HO, W8 = NC // 2, WY // 4, WY // 8
    AR, AC = PT + 2, PM + 2
    OR, OC = WY + 2, WX + 2
    WP = WX + 16
    XR = WY + 4
    HR_ = WY + 2
    FB = NLON // 4

    def kernel(
        atm, water, mask_h, oidx_h, ow_h, aidx_h, aw_h, fwt_h, flw_h, ipmt_h, drv_h, fb_h, ib_h, mw_h, filt_h,
        k1_h, k2_h, tab_h, tabt_h, atm_out, ocean_out,
        mask, oidx, ow, aidx, aw, fwt, flw, ipmt, drv, ya, us, st, drv3, wl, wr,
        atm_v, g1, tabt, tab, sp, rx, rxf, fb, ib, md, mp, mw, filt, qf, qb, vx, bx, gs, hh, lf, fbp, acc, ms,
        x, hl, hr, hd, w1, w2, oo,
        tf, ts, pf, ps, ef, es, efl, efr, esl, esr, rsc, csc, wsc, ss, sr, fx,
        ld, wsend, wrecv, csend, crecv, hsend, hrecv, g1s, g1r, sss, ssr, s2s, r2, mds, mdr,
        q_s, q_r, gss, gsr, hds, hdr, outs, shs, shr, fxs, fxr, ready,
    ):
        me = lax.axis_index("comp")
        row = lax.axis_index("row")
        col = lax.axis_index("col")
        flat = row * NC + col
        other = 1 - me

        def rmod(v):
            return lax.rem(v + NR, NR)

        def cmod(v):
            return lax.rem(v + NC, NC)

        def shifted(py, px):
            y = lax.rem(col // NX + py, NY)
            xx = lax.rem(lax.rem(col, NX) + px, NX)
            return y * NX + xx

        def partner(p):
            return rmod(row + lax.rem(p, NR)), shifted(p // (NR * NX), lax.rem(p // NR, NX))

        def send(src, dst, ssem, rsem, dev):
            pltpu.make_async_remote_copy(
                src_ref=src, dst_ref=dst, send_sem=ssem, recv_sem=rsem, device_id=dev, device_id_type=MESH
            ).start()

        def load(i, src, dst):
            pltpu.make_async_copy(src, dst, ld.at[i]).start()

        barrier = pltpu.get_barrier_semaphore()

        def greet(dev):
            pl.semaphore_signal(barrier, inc=1, device_id=dev, device_id_type=MESH)

        for d in range(1, NC):
            greet((me, row, cmod(col + d)))
        for d in range(1, NR):
            greet((me, rmod(row + d), col))
        for dr in (-1, 0, 1):
            for dc in (-1, 0, 1):
                greet((other, rmod(row + dr), cmod(col + dc)))
                if dr and dc:
                    greet((me, rmod(row + dr), cmod(col + dc)))

        load(1, water, x.at[me, 2 : 2 + WY, 0:WX])
        load(10, ipmt_h, ipmt)
        load(0, atm, atm_v)
        for n, (src, dst) in enumerate(
            ((fwt_h, fwt), (aidx_h, aidx), (aw_h, aw), (drv_h, drv), (mask_h, mask), (oidx_h, oidx), (ow_h, ow),
             (flw_h, flw))
        ):
            load(11 + n, src, dst)
        load(2, tabt_h, tabt)
        load(3, fb_h, fb)
        for a in range(3):
            for b in range(3):
                rows = pl.ds(a * 2 * CO, 2 * CO)
                cols = pl.ds(b * CO, CO)
                pltpu.make_async_copy(k1_h.at[a, b], w1.at[rows, cols], ld.at[8]).start()
                pltpu.make_async_copy(k2_h.at[a, b], w2.at[rows, cols], ld.at[9]).start()
        load(5, mw_h, mw)
        load(6, filt_h, filt)
        load(4, ib_h, ib)
        load(7, tab_h, tab)

        drain(x.at[0, 2 : 2 + WY, 0:WX], ld.at[1])
        drain(ipmt, ld.at[10])
        wv = x.at[me]

        def project_water(i, _):
            cells = wv[pl.ds(2 + 4 * i, 4), 0:WX, :].reshape(4 * WX, CO)
            got = dot_nt(ipmt[...], cells).astype(BF16)
            for j in range(4):
                ps[me, pl.ds((4 * i + j) * NF, NF), :] = got[:, j * WX : (j + 1) * WX]
            return 0

        lax.fori_loop(0, WY // 4, project_water, 0)
        sub = lax.broadcasted_iota(jnp.int32, (16, CO), 0)

        def pack_edges(j, _):
            left = jnp.zeros((16, CO), F32)
            right = jnp.zeros((16, CO), F32)
            for m in range(8):
                mine = (sub >= 2 * m) & (sub < 2 * m + 2)
                head = x[me, 2 + 8 * j + m, 0:16, :].astype(F32)
                tail = x[me, 2 + 8 * j + m, WX - 16 : WX, :].astype(F32)
                left = jnp.where(mine, pltpu.roll(head, 2 * m, 0), left)
                right = jnp.where(mine, pltpu.roll(tail, (2 * m + 2) % 16, 0), right)
            wl[j] = left.astype(BF16)
            wr[j] = right.astype(BF16)
            return 0

        pl.semaphore_wait(barrier, NC - 1 + NR - 1 + 9 + 4)
        for d in range(1, NR):
            pl.semaphore_signal(ready, inc=1, device_id=(me, rmod(row + d), col), device_id_type=MESH)

        send(ps.at[me], ps.at[me], csend.at[0], crecv.at[0], (other, row, col))

        def send_lat(t):
            pltpu.make_async_copy(atm.at[t * NC + col], g1.at[t, pl.ds(col * PM, PM)], g1r.at[t]).start()

            def step(p, _):
                there = shifted(p // NX, lax.rem(p, NX))
                send(
                    atm.at[t * NC + there], g1.at[t, pl.ds(col * PM, PM)], g1s.at[t], g1r.at[t], (me, row, there)
                )
                return 0

            lax.fori_loop(1, NC, step, 0)

        def water_sends(q):
            return [
                (row > 0, water.at[0:2], x.at[me, XR - 2 : XR, 0:WX], (q, rmod(row - 1), col)),
                (row < NR - 1, water.at[WY - 2 : WY], x.at[me, 0:2, 0:WX], (q, rmod(row + 1), col)),
                (col > 0, wl, hr.at[me, 0:W8], (q, row, cmod(col - 1))),
                (col < NC - 1, wr, hl.at[me, 0:W8], (q, row, cmod(col + 1))),
                ((row > 0) & (col > 0), wl.at[0], hr.at[me, W8 + 1], (q, rmod(row - 1), cmod(col - 1))),
                ((row > 0) & (col < NC - 1), wr.at[0], hl.at[me, W8 + 1], (q, rmod(row - 1), cmod(col + 1))),
                ((row < NR - 1) & (col > 0), wl.at[W8 - 1], hr.at[me, W8], (q, rmod(row + 1), cmod(col - 1))),
                ((row < NR - 1) & (col < NC - 1), wr.at[W8 - 1], hl.at[me, W8],
                 (q, rmod(row + 1), cmod(col + 1))),
            ]

        def water_recvs(q):
            return [
                (row < NR - 1, x.at[q, XR - 2 : XR, 0:WX]),
                (row > 0, x.at[q, 0:2, 0:WX]),
                (col < NC - 1, hr.at[q, 0:W8]),
                (col > 0, hl.at[q, 0:W8]),
                ((row < NR - 1) & (col < NC - 1), hr.at[q, W8 + 1]),
                ((row < NR - 1) & (col > 0), hl.at[q, W8 + 1]),
                ((row > 0) & (col < NC - 1), hr.at[q, W8]),
                ((row > 0) & (col > 0), hl.at[q, W8]),
            ]

        send_lat(0)

        def water_send(first, last):
            for q in range(2):
                for n, (there, src, dst, dev) in enumerate(water_sends(q)[first:last]):
                    @pl.when(there)
                    def _(src=src, dst=dst, dev=dev, n=n, q=q):
                        send(src, dst, wsend.at[first + n, q], wrecv.at[first + n, me], dev)

        water_send(0, 2)

        def both(part):
            return (part[0].astype(F32) + part[1].astype(F32)).astype(BF16)

        lane = lax.broadcasted_iota(jnp.int32, (16, 128), 1)
        line = lax.broadcasted_iota(jnp.int32, (16, 128), 0)

        def pick(cond):
            return jnp.where(cond, 1.0, 0.0).astype(BF16)

        def halo_parts(tab_ref, edge, left, right, rows):
            above = pl.ds((rows + 1) * NF, NF)
            below = pl.ds(rows * NF, NF)
            parts = [
                (row > 0, row < NR - 1, tab_ref.at[0:NF, 0:128], tab_ref.at[below, 0:128], (-1, 0)),
                (row < NR - 1, row > 0, tab_ref.at[(rows - 1) * NF : rows * NF, 0:128], tab_ref.at[above, 0:128],
                 (1, 0)),
            ]
            for dr in (-1, 0, 1):
                to = (row > 0) if dr < 0 else (row < NR - 1) if dr > 0 else (row >= 0)
                fro = (row < NR - 1) if dr < 0 else (row > 0) if dr > 0 else (row >= 0)
                parts.append((to & (col > 0), fro & (col < NC - 1), edge, right.at[1 - dr], (dr, -1)))
                parts.append((to & (col < NC - 1), fro & (col > 0), edge, left.at[1 - dr], (dr, 1)))
            return parts

        def halo_send(tab_ref, edge, left, right, rows, width, at):
            ends = pick(((line == 0) & (lane == 0)) | ((line == 1) & (lane == width - 1)))
            edge[...] = dot_nt(ends, tab_ref[0 : rows * NF, 0:128]).astype(BF16)
            for n, (to, _, src, dst, (dr, dc)) in enumerate(halo_parts(tab_ref, edge, left, right, rows)):
                @pl.when(to)
                def _(src=src, dst=dst, n=n, dr=dr, dc=dc):
                    send(src, dst, hsend.at[at + n], hrecv.at[at + n], (me, rmod(row + dr), cmod(col + dc)))

        def halo_recv(tab_ref, edge, left, right, rows, at):
            for n, (_, fro, src, dst, _) in enumerate(halo_parts(tab_ref, edge, left, right, rows)):
                @pl.when(fro)
                def _(dst=dst, n=n):
                    drain(dst, hrecv.at[at + n])

            @pl.when(row == NR - 1)
            def _():
                tab_ref[rows * NF : (rows + 1) * NF, 0:128] = jnp.zeros((NF, 128), BF16)

            @pl.when(row == 0)
            def _():
                tab_ref[(rows + 1) * NF : (rows + 2) * NF, 0:128] = jnp.zeros((NF, 128), BF16)

        def halo_sent(tab_ref, edge, left, right, rows, at, first, last):
            for n, (to, _, src, _, _) in enumerate(halo_parts(tab_ref, edge, left, right, rows)):
                if first <= n < last:
                    @pl.when(to)
                    def _(src=src, n=n):
                        drain(src, hsend.at[at + n])

        def halo_columns(left, right, rows, place):
            def column(got, inside):
                mid = jnp.where(inside, got[1].astype(F32), 0.0)
                below = jnp.where(inside & (row < NR - 1), got[2].astype(F32)[:, 0:NF], 0.0)
                above = jnp.where(inside & (row > 0), got[0].astype(F32)[:, (rows - 1) * NF : rows * NF], 0.0)
                return jnp.concatenate([mid, below, above], axis=1).astype(BF16)

            from_right = pick((line == 0) & (lane == place))
            from_left = pick((line == 1) & (lane == place + 1))
            return dot_tn(column(right, col < NC - 1), from_right) + dot_tn(column(left, col > 0), from_left)

        def regrid(tab_ref, index, weight, rows, cols, block):
            cells = index.astype(F32)
            r_at = jnp.floor((cells + 0.5) * (1.0 / cols))
            c_at = cells - r_at * cols
            rsc[...] = jnp.where(r_at == 0, rows - 1.0, r_at - 1.0)
            csc[...] = jnp.where(c_at == 0, cols - 1.0, c_at - 1.0)
            wsc[...] = weight / jnp.sum(weight, axis=0, keepdims=True)
            width = tab_ref.shape[1]
            at = lax.broadcasted_iota(jnp.int32, (width, LANES), 0).astype(F32)

            def source(k, total):
                r_k = rsc[pl.ds(k, 1), :]
                c_k = csc[pl.ds(k, 1), :]
                w_k = wsc[pl.ds(k, 1), :]
                chosen = jnp.where(at == c_k, 1.0, 0.0).astype(BF16)
                for b in range(rows // block):
                    lines = dot(tab_ref[b * block * NF : (b + 1) * block * NF, :], chosen)
                    for j in range(block):
                        share = jnp.where(r_k == float(b * block + j), w_k, 0.0)
                        total = total + lines[j * NF : (j + 1) * NF] * share
                return total

            return lax.fori_loop(0, 4, source, jnp.zeros((NF, LANES), F32))

        drain(ps.at[0], crecv.at[0])
        ts[0 : WY * NF, 0:128] = both(ps)
        halo_send(ts, es, esl, esr, WY, WX, 0)

        drain(atm_v, ld.at[0])
        drain(fwt, ld.at[11])

        def project_air(t, _):
            cells = atm_v[pl.ds(t * 4, 4)].reshape(4 * PM, C)
            got = dot_nt(fwt[...], cells)
            zeros = jnp.zeros((NF, 128 - PM), F32)
            for j in range(4):
                part = jnp.concatenate([got[:, j * PM : (j + 1) * PM], zeros], axis=1)
                pf[me, pl.ds((t * 4 + j) * NF, NF), :] = part.astype(BF16)
            return 0

        lax.fori_loop(0, PT // 4, project_air, 0)
        send(pf.at[me], pf.at[me], csend.at[1], crecv.at[1], (other, row, col))

        send_lat(1)
        halo_recv(ts, es, esl, esr, WY, 0)
        halo_sent(ts, es, esl, esr, WY, 0, 0, 2)
        ts[:, 128:256] = halo_columns(esl, esr, WY, 0).astype(BF16)

        for n, ref in ((12, aidx), (13, aw), (14, drv)):
            drain(ref, ld.at[n])

        def to_air(i, _):
            c = me * HC + i
            idx = jnp.concatenate(
                [aidx[t * NC + c] for t in range(LT)] + [jnp.zeros((4, LANES - LT * PM), jnp.int32)], axis=1
            )
            wgt = jnp.concatenate(
                [aw[t * NC + c] for t in range(LT)] + [jnp.ones((4, LANES - LT * PM), F32)], axis=1
            )
            ss[c] = regrid(ts, idx, wgt, OR, OC, 13 if OR % 13 == 0 else 1).astype(BF16)
            send(ss.at[c], sr.at[col], sss, ssr, (other, row, c))
            send(ss.at[c], ss.at[c], shs, shr, (other, row, col))

            @pl.when(c != col)
            def _():
                send(ss.at[c], sr.at[col], sss, ssr, (me, row, c))

            @pl.when(c == col)
            def _():
                pltpu.make_async_copy(ss.at[c], sr.at[col], ssr).start()

            return 0

        lax.fori_loop(0, HC, to_air, 0)
        send_lat(2)
        lax.fori_loop(0, W8, pack_edges, 0)
        water_send(2, 8)
        send(water, x.at[me, 2 : 2 + WY, 0:WX], wsend.at[8, 0], wrecv.at[8, 0], (other, row, col))
        drain(pf.at[0], crecv.at[1])
        tf[0 : PT * NF, :] = both(pf)
        halo_send(tf, ef, efl, efr, PT, PM, 8)

        drain(tabt, ld.at[2])

        for t in range(LT):
            drain(g1.at[t], g1r.at[t])

            def analyse(b, _, t=t):
                rows = pl.ds(pl.multiple_of(b * FB, FB), FB)
                ya[t, rows, :] = dot(tabt[rows, :], g1[t])
                return 0

            lax.fori_loop(0, 4, analyse, 0)

        drv3[...] = jnp.zeros(drv3.shape, BF16)
        for t in range(LT):
            drv3[t, t * NF : (t + 1) * NF, :] = drv[...]
        drain(sr, ssr)
        for t in range(LT):
            st[t * NF : (t + 1) * NF, :] = jnp.concatenate(
                [sr[c].astype(F32)[:, t * PM : (t + 1) * PM] for c in range(NC)], axis=1
            ).astype(BF16)

        def analyse_fields(b, _):
            rows = pl.ds(pl.multiple_of(b * FB, FB), FB)
            us[rows, :] = dot_nt(tabt[rows, :], st[...]).astype(BF16)
            return 0

        lax.fori_loop(0, 4, analyse_fields, 0)
        pl.semaphore_wait(ready, NR - 1)

        HALVES = ((1, ND // 2), (ND // 2, ND))

        def scatter(t, h):
            if h == 0:
                pltpu.make_async_copy(sp.at[t, flat], rx.at[t, flat], r2.at[t]).start()

            def step(p, _):
                r_to, c_to = partner(p)
                send(sp.at[t, r_to * NC + c_to], rx.at[t, flat], s2s.at[t, h], r2.at[t], (me, r_to, c_to))
                return 0

            lax.fori_loop(*HALVES[h], step, 0)

        def scattered(t, h):
            drain(sp.at[t, 0 : HALVES[h][1] - HALVES[h][0]], s2s.at[t, h])

        def force(t):
            def step(b, _):
                rows = pl.ds(pl.multiple_of(b * FB, FB), FB)
                got = ya[t, rows, :] + dot(us[rows, :], drv3[t])
                halves = [got[:, h * 128 : (h + 1) * 128].reshape(FB // 8, 8, 128) for h in range(2)]
                sp[t, pl.ds(b * (FB // 8), FB // 8)] = jnp.concatenate(halves, axis=1).astype(BF16)
                return 0

            lax.fori_loop(0, 4, step, 0)

        force(0)
        scatter(0, 0)
        scatter(0, 1)
        for t in range(1, LT):
            force(t)

        drain(ss.at[0:HC], shr)

        def lift_here(c, _):
            term = dot_tn(ss[c], drv[...])
            for t in range(LT):
                n = t * NC + c
                lf[n] = (atm_v[n].astype(F32) + term[t * PM : (t + 1) * PM]).astype(BF16)
            return 0

        lax.fori_loop(0, NC, lift_here, 0)

        scattered(0, 0)
        scatter(1, 0)

        drain(fb, ld.at[3])
        lat_in = lax.broadcasted_iota(jnp.int32, (NLAT, NLAT), 0)
        lat_to = lax.broadcasted_iota(jnp.int32, (NLAT, NLAT), 1)
        t_to, d_to = lat_to // ND, lax.rem(lat_to, ND)
        order = pick(lat_in == (d_to // NC) * PT + t_to * NC + lax.rem(d_to, NC))

        def reorder(k, _):
            fbp[k] = dot(fb[k], order).astype(BF16)
            return 0

        lax.fori_loop(0, KB, reorder, 0)
        scattered(0, 1)
        scatter(1, 1)

        halo_recv(tf, ef, efl, efr, PT, 8)
        halo_sent(tf, ef, efl, efr, PT, 8, 0, 2)
        tf[...] = (tf[...].astype(F32) + halo_columns(efl, efr, PT, PM)).astype(BF16)

        for n, ref in ((15, mask), (16, oidx), (17, ow), (18, flw)):
            drain(ref, ld.at[n])

        def to_ocean(j, _):
            i = me * HO + j
            idx = jnp.concatenate([oidx[2 * i], oidx[2 * i + 1]], axis=1)
            wgt = jnp.concatenate([ow[2 * i], ow[2 * i + 1]], axis=1)
            fx[i] = regrid(tf, idx, wgt, AR, AC, 10 if AR % 10 == 0 else 1).astype(BF16)
            send(fx.at[i], fx.at[i], fxs, fxr, (other, row, col))
            return 0

        lax.fori_loop(0, HO, to_ocean, 0)
        scattered(1, 0)
        scatter(2, 0)

        for q in range(2):
            for n, (there, dst) in enumerate(water_recvs(q)):
                @pl.when(there)
                def _(dst=dst, n=n, q=q):
                    drain(dst, wrecv.at[n, q])
        drain(x.at[0, 2 : 2 + WY, 0:WX], wrecv.at[8, 0])

        @pl.when(row == 0)
        def _():
            x[:, 0:2, 0:WX, :] = jnp.zeros((2, 2, WX, CO), BF16)

        @pl.when(row == NR - 1)
        def _():
            x[:, XR - 2 : XR, 0:WX, :] = jnp.zeros((2, 2, WX, CO), BF16)

        def side(i, tile, m, inside):
            for q in range(2):
                from_right = pltpu.roll(hr[q, tile].astype(F32), (16 - 2 * m) % 16, 0)
                from_left = pltpu.roll(hl[q, tile].astype(F32), (30 - 2 * m) % 16, 0)
                cells = jnp.where(
                    (sub < 2) & inside & (col < NC - 1),
                    from_right,
                    jnp.where((sub >= 14) & inside & (col > 0), from_left, 0.0),
                )
                x[q, i, WX:WP, :] = cells.astype(BF16)

        def sides(j, _):
            for m in range(8):
                side(2 + 8 * j + m, j, m, True)
            return 0

        lax.fori_loop(0, W8, sides, 0)
        for m in range(2):
            side(m, W8, 6 + m, row > 0)
            side(XR - 2 + m, W8 + 1, m, row < NR - 1)
        drain(w1, ld.at[8])

        def taps(src, weight, first, count):
            lhs = jnp.concatenate(
                [
                    jnp.concatenate([src[q, first + j + a] for a in range(3) for q in range(2)], axis=1)
                    for j in range(count)
                ],
                axis=0,
            )
            got = dot(lhs, weight[...])
            outs_ = []
            for j in range(count):
                part = got[j * WP : (j + 1) * WP]
                outs_.append(
                    pltpu.roll(part[:, 0:CO], 1, 0)
                    + part[:, CO : 2 * CO]
                    + pltpu.roll(part[:, 2 * CO : 3 * CO], WP - 1, 0)
                )
            return outs_

        def conv_first(i, _):
            place = lax.broadcasted_iota(jnp.int32, (WP, CO), 0)
            edge = ((place == WP - 1) & (col == 0)) | ((place == WX) & (col == NC - 1))
            for j, out in enumerate(taps(x, w1, 2 * i, 2)):
                h = 2 * i + j
                outside = ((h == 0) & (row == 0)) | ((h == HR_ - 1) & (row == NR - 1))
                hd[me, h] = jnp.where(edge | outside, 0.0, gelu(out)).astype(BF16)
            return 0

        lax.fori_loop(0, HR_ // 2, conv_first, 0)
        send(hd.at[me], hd.at[me], hds, hdr, (other, row, col))

        scattered(1, 1)
        scatter(2, 1)

        TB = 32 if ND % 32 == 0 else 8

        def widen(t):
            drain(rx.at[t], r2.at[t])

            def step(i, _):
                rows = pl.ds(pl.multiple_of(i * TB, TB), TB)
                out_rows = pl.ds(pl.multiple_of((t * ND + i * TB) * 16, TB * 16), TB * 16)
                rxf[out_rows, :] = rx[t, rows].astype(F32).reshape(TB * 16, 128)
                return 0

            lax.fori_loop(0, ND // TB, step, 0)

        def spectra_of(k, first, last):
            count = (last - first) * ND
            return jnp.concatenate(
                [rxf[pl.ds(first * ND * 16 + k + 8 * h, count, stride=16), :] for h in range(2)], axis=1
            ).astype(BF16)

        for t in range(LT - 1):
            widen(t)
        SPLIT = (LT - 1) * ND

        def to_modes_first(k, _):
            acc[k] = dot(fbp[k, :, 0:SPLIT], spectra_of(k, 0, LT - 1))
            return 0

        lax.fori_loop(0, KB, to_modes_first, 0)
        drain(mw, ld.at[5])
        drain(filt, ld.at[6])
        drain(ib, ld.at[4])
        widen(LT - 1)

        def to_modes(k, _):
            md[k] = (acc[k] + dot(fbp[k, :, SPLIT:NLAT], spectra_of(k, LT - 1, LT))).astype(BF16)
            send(md.at[k], mp.at[k], mds.at[k], mdr.at[k], (other, row, col))
            return 0

        lax.fori_loop(0, KB, to_modes, 0)

        def mix_own(k, _):
            acc[k] = dot(md[k], mw[pl.ds(pl.multiple_of(me * C, C), C), :])
            return 0

        lax.fori_loop(0, KB, mix_own, 0)

        def mix(k, _):
            drain(mp.at[k], mdr.at[k])
            mixed = acc[k] + dot(mp[k], mw[pl.ds(pl.multiple_of(other * C, C), C), :])
            ms[k] = (mixed * filt[...]).astype(BF16)
            return 0

        lax.fori_loop(0, KB, mix, 0)

        def gather_back(t, h):
            if h == 0:
                pltpu.make_async_copy(qb.at[t, flat], vx.at[t, flat], q_r.at[t]).start()

            def step(p, _):
                r_to, c_to = partner(p)
                send(qb.at[t, r_to * NC + c_to], vx.at[t, flat], q_s.at[t, h], q_r.at[t], (me, r_to, c_to))
                return 0

            lax.fori_loop(*HALVES[h], step, 0)

        def gathered(t, h):
            drain(vx.at[t, 0 : HALVES[h][1] - HALVES[h][0]], q_s.at[t, h])

        def synth(t):
            def to_synth(k, _):
                basis = ib[k].reshape(NR, LT, NC, DEG)[:, t].reshape(ND, DEG)
                got = dot(basis, ms[k])
                for h in range(2):
                    qf[pl.ds(k + 8 * h, ND, stride=16), :] = got[:, h * 128 : (h + 1) * 128]
                return 0

            lax.fori_loop(0, KB, to_synth, 0)

            def narrow(i, _):
                rows = pl.ds(pl.multiple_of(i * TB, TB), TB)
                in_rows = pl.ds(pl.multiple_of(i * TB * 16, TB * 16), TB * 16)
                qb[t, rows] = qf[in_rows, :].reshape(TB, 16, 128).astype(BF16)
                return 0

            lax.fori_loop(0, ND // TB, narrow, 0)

        synth(0)
        gather_back(0, 0)
        gather_back(0, 1)
        synth(1)
        gathered(0, 0)
        gather_back(1, 0)
        synth(2)
        gathered(0, 1)
        gather_back(1, 1)

        drain(hd.at[0], hdr)
        drain(fx.at[0:HO], fxr)
        drain(w2, ld.at[9])

        def conv_second(i, _):
            outs_ = taps(hd, w2, 2 * i, 2)
            sixteenth = jnp.full((NF, CO), 1.0 / NF, BF16)
            for j in range(2):
                r = 2 * i + j
                lift = dot_tn(fx[i, :, j * WX : (j + 1) * WX], flw[...])
                line_mask = jnp.broadcast_to(mask[pl.ds(r, 1), :].astype(F32), (NF, WX)).astype(BF16)
                keep = dot_tn(line_mask, sixteenth)
                here = x[me, r + 2, 0:WX, :].astype(F32)
                oo[r] = (here + keep * (outs_[j][0:WX] + lift)).astype(BF16)
            return 0

        lax.fori_loop(0, WY // 2, conv_second, 0)
        pltpu.make_async_copy(oo, ocean_out, outs.at[0]).start()
        gathered(1, 0)
        gather_back(2, 0)

        drain(tab, ld.at[7])
        def to_grid(t):
            drain(vx.at[t], q_r.at[t])
            for h in range(2):
                part = vx[t].astype(F32)[:, 8 * h : 8 * h + 8, :].reshape(NLON, 128)
                bx[:, h * 128 : (h + 1) * 128] = part.astype(BF16)

            def synthesise(b, _):
                y = lax.rem(col // NX + b, NY)
                rows = pl.ds(pl.multiple_of(y * NX * PM, NX * PM), NX * PM)
                gs[t, rows, :] = dot(tab[rows, :], bx[...]).astype(BF16)

                def home(p, _):
                    there = y * NX + lax.rem(lax.rem(col, NX) + p, NX)

                    @pl.when(there != col)
                    def _():
                        send(gs.at[t, pl.ds(there * PM, PM)], hh.at[t * NC + col], gss.at[t], gsr.at[t],
                             (me, row, there))

                    @pl.when(there == col)
                    def _():
                        pltpu.make_async_copy(
                            gs.at[t, pl.ds(col * PM, PM)], hh.at[t * NC + col], gsr.at[t]
                        ).start()

                    return 0

                lax.fori_loop(0, NX, home, 0)
                return 0

            lax.fori_loop(0, NY, synthesise, 0)

        def finish_lats(t):
            drain(hh.at[t * NC : (t + 1) * NC], gsr.at[t])

            def finish(c, _):
                n = t * NC + c
                lf[n] = (lf[n].astype(F32) + gelu(hh[n].astype(F32))).astype(BF16)
                return 0

            lax.fori_loop(0, NC, finish, 0)
            done = pl.ds(t * NC, NC)
            pltpu.make_async_copy(lf.at[done], atm_out.at[done], outs.at[1]).start()

        to_grid(0)
        gathered(1, 1)
        gather_back(2, 1)
        to_grid(1)
        finish_lats(0)
        to_grid(2)
        finish_lats(1)
        finish_lats(2)

        for t in range(LT):
            drain(g1.at[t, 0 : (NC - 1) * PM], g1s.at[t])
            drain(gs.at[t, 0 : (NC - 1) * PM], gss.at[t])
        for h in range(2):
            scattered(LT - 1, h)
            gathered(LT - 1, h)
        drain(sr.at[0 : NC - 1], sss)

        @pl.when((col < me * HC) | (col >= me * HC + HC))
        def _():
            drain(sr.at[0], sss)

        drain(ss.at[0:HC], shs)
        drain(fx.at[0:HO], fxs)
        for q in range(2):
            for n, (there, src, dst, dev) in enumerate(water_sends(q)):
                @pl.when(there)
                def _(src=src, n=n, q=q):
                    drain(src, wsend.at[n, q])
        drain(water, wsend.at[8, 0])
        drain(ps.at[0], csend.at[0])
        drain(pf.at[0], csend.at[1])
        drain(hd.at[0], hds)
        for k in range(KB):
            drain(mp.at[k], mds.at[k])
        halo_sent(ts, es, esl, esr, WY, 0, 2, 8)
        halo_sent(tf, ef, efl, efr, PT, 8, 2, 8)
        drain(oo, outs.at[0])
        drain(lf, outs.at[1])

    v = pltpu.VMEM
    dma = pltpu.SemaphoreType.DMA
    scratch = [
        v((WY, WX), jnp.int32), v((WY, 4, WX), jnp.int32), v((WY, 4, WX), F32), v((PT, 4, PM), jnp.int32),
        v((PT, 4, PM), F32), v((NF, C), BF16), v((NF, CO), BF16), v((NF, CO), BF16), v((NF, C), BF16),
        v((LT, NLON, C), F32), v((NLON, LT * NF), BF16), v((LT * NF, NLON), BF16), v((LT, LT * NF, C), BF16),
        v((W8, 16, CO), BF16), v((W8, 16, CO), BF16),
        v((PT, PM, C), BF16), v((LT, NLON, C), BF16), v((NLON, NLON), BF16), v((NLON, NLON), BF16),
        v((LT, ND, 16, 128), BF16), v((LT, ND, 16, 128), BF16), v((NLAT * 16, 128), F32),
        v((KB, DEG, NLAT), BF16), v((KB, NLAT, DEG), BF16), v((KB, DEG, C), BF16), v((KB, DEG, C), BF16),
        v((2 * C, C), BF16), v((DEG, C), F32), v((ND * 16, 128), F32), v((LT, ND, 16, 128), BF16),
        v((LT, ND, 16, 128), BF16), v((NLON, C), BF16), v((LT, NLON, C), BF16), v((PT, PM, C), BF16), v((PT, PM, C), BF16),
        v((KB, DEG, NLAT), BF16), v((KB, DEG, C), F32), v((KB, DEG, C), BF16),
        v((2, XR, WP, CO), BF16), v((2, W8 + 2, 16, CO), BF16), v((2, W8 + 2, 16, CO), BF16), v((2, HR_, WP, CO), BF16),
        v((6 * CO, 3 * CO), BF16), v((6 * CO, 3 * CO), BF16), v((WY, WX, CO), BF16),
        v((AR * NF, 128), BF16), v((OR * NF, 256), BF16), v((2, PT * NF, 128), BF16), v((2, WY * NF, 128), BF16),
        v((16, PT * NF), BF16), v((16, WY * NF), BF16),
        v((3, 16, PT * NF), BF16), v((3, 16, PT * NF), BF16), v((3, 16, WY * NF), BF16), v((3, 16, WY * NF), BF16),
        v((4, LANES), F32), v((4, LANES), F32), v((4, LANES), F32),
        v((NC, NF, LANES), BF16), v((NC, NF, LANES), BF16), v((WY // 2, NF, LANES), BF16),
        dma((19,)), dma((9, 2)), dma((9, 2)), dma((2,)), dma((2,)), dma((16,)), dma((16,)),
        dma((LT,)), dma((LT,)), dma, dma, dma((LT, 2)), dma((LT,)), dma((KB,)), dma((KB,)),
        dma((LT, 2)), dma((LT,)), dma((LT,)), dma((LT,)), dma, dma, dma((2,)), dma, dma, dma, dma, pltpu.SemaphoreType.REGULAR,
    ]
    any_ = pl.BlockSpec(memory_space=pl.ANY)
    return pl.pallas_call(
        kernel,
        out_shape=(
            jax.ShapeDtypeStruct((PT, PM, C), BF16),
            jax.ShapeDtypeStruct((WY, WX, CO), BF16),
        ),
        in_specs=[any_] * 19,
        out_specs=(any_, any_),
        scratch_shapes=scratch,
        compiler_params=pltpu.CompilerParams(
            collective_id=0, has_side_effects=True, vmem_limit_bytes=60 * 1024 * 1024
        ),
        cost_estimate=pl.CostEstimate(flops=9_000_000_000, bytes_accessed=20_000_000, transcendentals=2_000_000),
        name="coupled_step",
    )


def settle(*arrays):
    pieces = 4
    count = len(arrays)

    def kernel(*refs):
        for n in range(count):
            refs[count + n][...] = refs[n][...]

    specs = [
        pl.BlockSpec((a.shape[0] // pieces,) + a.shape[1:], lambda i: (i, 0, 0)) for a in arrays
    ]
    return pl.pallas_call(
        kernel,
        out_shape=tuple(jax.ShapeDtypeStruct(a.shape, a.dtype) for a in arrays),
        grid=(pieces,),
        in_specs=specs,
        out_specs=tuple(specs),
        compiler_params=pltpu.CompilerParams(vmem_limit_bytes=32 * 1024 * 1024),
        name="settle",
    )(*arrays)


def solution(mesh):
    NR, NC = mesh.shape["row"], mesh.shape["col"]
    NX = 4 if NC == 16 else NC

    def local(
        atmosphere_state, water_condition, ocean_cell_mask, atmos_to_ocean_index, atmos_to_ocean_weight,
        water_source_positions, water_source_overlay_areas, flux_weight, flux_lift_weight,
        interface_projection_matrix, interface_driving_matrix, forward_basis, inverse_basis,
        mixing_weight, degree_filter, first_ocean_kernel, second_ocean_kernel,
    ):
        PT, PM, C = atmosphere_state.shape
        WY, WX, CO = water_condition.shape
        table = lon_table(NC * PM)
        step = make_kernel(
            NR, NC, NX, PT, PM, C, WY, WX, CO, flux_weight.shape[1], forward_basis.shape[1]
        )
        return settle(*step(
            atmosphere_state,
            water_condition,
            ocean_cell_mask,
            jnp.swapaxes(atmos_to_ocean_index, 1, 2),
            jnp.swapaxes(atmos_to_ocean_weight, 1, 2),
            jnp.swapaxes(water_source_positions, 1, 2),
            jnp.swapaxes(water_source_overlay_areas, 1, 2),
            flux_weight.T,
            flux_lift_weight,
            interface_projection_matrix.T,
            interface_driving_matrix,
            forward_basis,
            inverse_basis,
            mixing_weight,
            degree_filter,
            first_ocean_kernel,
            second_ocean_kernel,
            jnp.asarray(table),
            jnp.asarray(np.ascontiguousarray(table.T)),
        ))

    placed = (
        P("row", "col", "comp"),
        P("row", "col", "comp"),
        P("row", "col"),
        P("row", "col", None),
        P("row", "col", None),
        P("row", "col", None),
        P("row", "col", None),
        P("comp", None),
        P(None, "comp"),
        P("comp", None),
        P(None, "comp"),
        P(("row", "col"), None, None),
        P(("row", "col"), None, None),
        P(None, "comp"),
        P(None, "comp"),
        P(None, None, None, "comp"),
        P(None, None, None, "comp"),
    )
    return jax.shard_map(
        local,
        mesh=mesh,
        in_specs=placed,
        out_specs=(P("row", "col", "comp"), P("row", "col", "comp")),
        check_vma=False,
    )
```

```python
import math

import jax
import jax.numpy as jnp
import ml_dtypes
import numpy as np
from jax import lax
from jax.experimental import pallas as pl
from jax.experimental.pallas import tpu as pltpu
from jax.sharding import PartitionSpec as P

BF16 = jnp.bfloat16
F32 = jnp.float32
MESH = pl.DeviceIdType.MESH
LANES = 256


def lon_table(count):
    col_idx = np.arange(count, dtype=np.int64)[:, None]
    coef_idx = np.arange(count, dtype=np.int64)[None, :]
    half_count = count // 2
    freq = np.where(coef_idx <= half_count, coef_idx, coef_idx - half_count)
    phase = (col_idx * freq % count) * (2.0 * math.pi / count)
    values = np.where(coef_idx <= half_count, np.cos(phase), np.sin(phase))
    return (values * math.sqrt(2.0 / count)).astype(ml_dtypes.bfloat16)


def dot(a, b):
    return jnp.dot(a, b, preferred_element_type=F32)


def dot_nt(a, b):
    return lax.dot_general(a, b, (((1,), (1,)), ((), ())), preferred_element_type=F32)


def dot_tn(a, b):
    return lax.dot_general(a, b, (((0,), (0,)), ((), ())), preferred_element_type=F32)


def drain(ref, sem):
    pltpu.make_async_copy(ref, ref, sem).wait()


def gelu(x):
    return jax.nn.gelu(x, approximate=True)


def make_kernel(NR, NC, NX, PT, PM, C, WY, WX, CO, NF, DEG):
    LT = PT // NC
    NLON = NC * PM
    ND = NR * NC
    KB = NLON // ND
    NLAT = NR * PT
    NY = NC // NX
    HC, HO, W8 = NC // 2, WY // 4, WY // 8
    AR, AC = PT + 2, PM + 2
    OR, OC = WY + 2, WX + 2
    WP = WX + 16
    XR = WY + 4
    HR_ = WY + 2
    FB = NLON // 4

    def kernel(
        atm, water, mask_h, oidx_h, ow_h, aidx_h, aw_h, fwt_h, flw_h, ipmt_h, drv_h, fb_h, ib_h, mw_h, filt_h,
        k1_h, k2_h, tab_h, tabt_h, atm_out, ocean_out,
        mask, oidx, ow, aidx, aw, fwt, flw, ipmt, drv, ya, us, st, drv3, wl, wr,
        atm_v, g1, tabt, tab, sp, rx, rxf, fb, ib, md, mp, mw, filt, qf, qb, vx, bx, gs, hh, lf, fbp, acc, ms,
        x, hl, hr, hd, w1, w2, oo,
        tf, ts, pf, ps, ef, es, efl, efr, esl, esr, rsc, csc, wsc, ss, sr, fx,
        ld, wsend, wrecv, csend, crecv, hsend, hrecv, g1s, g1r, sss, ssr, s2s, r2, mds, mdr,
        q_s, q_r, gss, gsr, hds, hdr, outs, shs, shr, fxs, fxr, ready,
    ):
        me = lax.axis_index("comp")
        row = lax.axis_index("row")
        col = lax.axis_index("col")
        flat = row * NC + col
        other = 1 - me

        def rmod(v):
            return lax.rem(v + NR, NR)

        def cmod(v):
            return lax.rem(v + NC, NC)

        def shifted(py, px):
            y = lax.rem(col // NX + py, NY)
            xx = lax.rem(lax.rem(col, NX) + px, NX)
            return y * NX + xx

        def all_partners(half, start):
            def line_of(c_to, first):
                for d in range(first, NR):
                    r_to = row + d
                    start(jnp.where(r_to >= NR, r_to - NR, r_to), c_to)

            if half == 0:
                line_of(col, 1)

            def step(p, _):
                line_of(shifted(p // NX, lax.rem(p, NX)), 0)
                return 0

            lax.fori_loop(1 if half == 0 else NC // 2, NC // 2 if half == 0 else NC, step, 0)

        def send(src, dst, ssem, rsem, dev):
            pltpu.make_async_remote_copy(
                src_ref=src, dst_ref=dst, send_sem=ssem, recv_sem=rsem, device_id=dev, device_id_type=MESH
            ).start()

        def load(i, src, dst):
            pltpu.make_async_copy(src, dst, ld.at[i]).start()

        barrier = pltpu.get_barrier_semaphore()

        def greet(dev):
            pl.semaphore_signal(barrier, inc=1, device_id=dev, device_id_type=MESH)

        for d in range(1, NC):
            greet((me, row, cmod(col + d)))
        for d in range(1, NR):
            greet((me, rmod(row + d), col))
        for dr in (-1, 0, 1):
            for dc in (-1, 0, 1):
                greet((other, rmod(row + dr), cmod(col + dc)))
                if dr and dc:
                    greet((me, rmod(row + dr), cmod(col + dc)))

        load(1, water, x.at[me, 2 : 2 + WY, 0:WX])
        load(10, ipmt_h, ipmt)
        load(0, atm, atm_v)
        for n, (src, dst) in enumerate(
            ((fwt_h, fwt), (aidx_h, aidx), (aw_h, aw), (drv_h, drv), (mask_h, mask), (oidx_h, oidx), (ow_h, ow),
             (flw_h, flw))
        ):
            load(11 + n, src, dst)
        load(2, tabt_h, tabt)
        load(3, fb_h, fb)
        for a in range(3):
            for b in range(3):
                rows = pl.ds(a * 2 * CO, 2 * CO)
                cols = pl.ds(b * CO, CO)
                pltpu.make_async_copy(k1_h.at[a, b], w1.at[rows, cols], ld.at[8]).start()
                pltpu.make_async_copy(k2_h.at[a, b], w2.at[rows, cols], ld.at[9]).start()
        load(5, mw_h, mw)
        load(6, filt_h, filt)
        load(4, ib_h, ib)
        load(7, tab_h, tab)

        drain(x.at[0, 2 : 2 + WY, 0:WX], ld.at[1])
        drain(ipmt, ld.at[10])
        wv = x.at[me]

        def project_water(i, _):
            cells = wv[pl.ds(2 + 4 * i, 4), 0:WX, :].reshape(4 * WX, CO)
            got = dot_nt(ipmt[...], cells).astype(BF16)
            for j in range(4):
                ps[me, pl.ds((4 * i + j) * NF, NF), :] = got[:, j * WX : (j + 1) * WX]
            return 0

        lax.fori_loop(0, WY // 4, project_water, 0)
        sub = lax.broadcasted_iota(jnp.int32, (16, CO), 0)

        def pack_edges(j, _):
            left = jnp.zeros((16, CO), F32)
            right = jnp.zeros((16, CO), F32)
            for m in range(8):
                mine = (sub >= 2 * m) & (sub < 2 * m + 2)
                head = x[me, 2 + 8 * j + m, 0:16, :].astype(F32)
                tail = x[me, 2 + 8 * j + m, WX - 16 : WX, :].astype(F32)
                left = jnp.where(mine, pltpu.roll(head, 2 * m, 0), left)
                right = jnp.where(mine, pltpu.roll(tail, (2 * m + 2) % 16, 0), right)
            wl[j] = left.astype(BF16)
            wr[j] = right.astype(BF16)
            return 0

        pl.semaphore_wait(barrier, NC - 1 + NR - 1 + 9 + 4)
        for d in range(1, NR):
            pl.semaphore_signal(ready, inc=1, device_id=(me, rmod(row + d), col), device_id_type=MESH)

        send(ps.at[me], ps.at[me], csend.at[0], crecv.at[0], (other, row, col))

        def send_lat(t):
            pltpu.make_async_copy(atm.at[t * NC + col], g1.at[t, pl.ds(col * PM, PM)], g1r.at[t]).start()

            def step(p, _):
                there = shifted(p // NX, lax.rem(p, NX))
                send(
                    atm.at[t * NC + there], g1.at[t, pl.ds(col * PM, PM)], g1s.at[t], g1r.at[t], (me, row, there)
                )
                return 0

            lax.fori_loop(1, NC, step, 0)

        def water_sends(q):
            return [
                (row > 0, water.at[0:2], x.at[me, XR - 2 : XR, 0:WX], (q, rmod(row - 1), col)),
                (row < NR - 1, water.at[WY - 2 : WY], x.at[me, 0:2, 0:WX], (q, rmod(row + 1), col)),
                (col > 0, wl, hr.at[me, 0:W8], (q, row, cmod(col - 1))),
                (col < NC - 1, wr, hl.at[me, 0:W8], (q, row, cmod(col + 1))),
                ((row > 0) & (col > 0), wl.at[0], hr.at[me, W8 + 1], (q, rmod(row - 1), cmod(col - 1))),
                ((row > 0) & (col < NC - 1), wr.at[0], hl.at[me, W8 + 1], (q, rmod(row - 1), cmod(col + 1))),
                ((row < NR - 1) & (col > 0), wl.at[W8 - 1], hr.at[me, W8], (q, rmod(row + 1), cmod(col - 1))),
                ((row < NR - 1) & (col < NC - 1), wr.at[W8 - 1], hl.at[me, W8],
                 (q, rmod(row + 1), cmod(col + 1))),
            ]

        def water_recvs(q):
            return [
                (row < NR - 1, x.at[q, XR - 2 : XR, 0:WX]),
                (row > 0, x.at[q, 0:2, 0:WX]),
                (col < NC - 1, hr.at[q, 0:W8]),
                (col > 0, hl.at[q, 0:W8]),
                ((row < NR - 1) & (col < NC - 1), hr.at[q, W8 + 1]),
                ((row < NR - 1) & (col > 0), hl.at[q, W8 + 1]),
                ((row > 0) & (col < NC - 1), hr.at[q, W8]),
                ((row > 0) & (col > 0), hl.at[q, W8]),
            ]

        def water_send(first, last):
            for q in range(2):
                for n, (there, src, dst, dev) in enumerate(water_sends(q)[first:last]):
                    @pl.when(there)
                    def _(src=src, dst=dst, dev=dev, n=n, q=q):
                        send(src, dst, wsend.at[first + n, q], wrecv.at[first + n, me], dev)


        def both(part):
            return (part[0].astype(F32) + part[1].astype(F32)).astype(BF16)

        lane = lax.broadcasted_iota(jnp.int32, (16, 128), 1)
        line = lax.broadcasted_iota(jnp.int32, (16, 128), 0)

        def pick(cond):
            return jnp.where(cond, 1.0, 0.0).astype(BF16)

        def halo_parts(tab_ref, edge, left, right, rows):
            above = pl.ds((rows + 1) * NF, NF)
            below = pl.ds(rows * NF, NF)
            parts = [
                (row > 0, row < NR - 1, tab_ref.at[0:NF, 0:128], tab_ref.at[below, 0:128], (-1, 0)),
                (row < NR - 1, row > 0, tab_ref.at[(rows - 1) * NF : rows * NF, 0:128], tab_ref.at[above, 0:128],
                 (1, 0)),
            ]
            for dr in (-1, 0, 1):
                to = (row > 0) if dr < 0 else (row < NR - 1) if dr > 0 else (row >= 0)
                fro = (row < NR - 1) if dr < 0 else (row > 0) if dr > 0 else (row >= 0)
                parts.append((to & (col > 0), fro & (col < NC - 1), edge, right.at[1 - dr], (dr, -1)))
                parts.append((to & (col < NC - 1), fro & (col > 0), edge, left.at[1 - dr], (dr, 1)))
            return parts

        def halo_send(tab_ref, edge, left, right, rows, width, at):
            ends = pick(((line == 0) & (lane == 0)) | ((line == 1) & (lane == width - 1)))
            edge[...] = dot_nt(ends, tab_ref[0 : rows * NF, 0:128]).astype(BF16)
            for n, (to, _, src, dst, (dr, dc)) in enumerate(halo_parts(tab_ref, edge, left, right, rows)):
                @pl.when(to)
                def _(src=src, dst=dst, n=n, dr=dr, dc=dc):
                    send(src, dst, hsend.at[at + n], hrecv.at[at + n], (me, rmod(row + dr), cmod(col + dc)))

        def halo_recv(tab_ref, edge, left, right, rows, at):
            for n, (_, fro, src, dst, _) in enumerate(halo_parts(tab_ref, edge, left, right, rows)):
                @pl.when(fro)
                def _(dst=dst, n=n):
                    drain(dst, hrecv.at[at + n])

            @pl.when(row == NR - 1)
            def _():
                tab_ref[rows * NF : (rows + 1) * NF, 0:128] = jnp.zeros((NF, 128), BF16)

            @pl.when(row == 0)
            def _():
                tab_ref[(rows + 1) * NF : (rows + 2) * NF, 0:128] = jnp.zeros((NF, 128), BF16)

        def halo_sent(tab_ref, edge, left, right, rows, at, first, last):
            for n, (to, _, src, _, _) in enumerate(halo_parts(tab_ref, edge, left, right, rows)):
                if first <= n < last:
                    @pl.when(to)
                    def _(src=src, n=n):
                        drain(src, hsend.at[at + n])

        def halo_columns(left, right, rows, place):
            def column(got, inside):
                mid = jnp.where(inside, got[1].astype(F32), 0.0)
                below = jnp.where(inside & (row < NR - 1), got[2].astype(F32)[:, 0:NF], 0.0)
                above = jnp.where(inside & (row > 0), got[0].astype(F32)[:, (rows - 1) * NF : rows * NF], 0.0)
                return jnp.concatenate([mid, below, above], axis=1).astype(BF16)

            from_right = pick((line == 0) & (lane == place))
            from_left = pick((line == 1) & (lane == place + 1))
            return dot_tn(column(right, col < NC - 1), from_right) + dot_tn(column(left, col > 0), from_left)

        def regrid(tab_ref, index, weight, rows, cols, block):
            cells = index.astype(F32)
            r_at = jnp.floor((cells + 0.5) * (1.0 / cols))
            c_at = cells - r_at * cols
            rsc[...] = jnp.where(r_at == 0, rows - 1.0, r_at - 1.0)
            csc[...] = jnp.where(c_at == 0, cols - 1.0, c_at - 1.0)
            wsc[...] = weight / jnp.sum(weight, axis=0, keepdims=True)
            width = tab_ref.shape[1]
            at = lax.broadcasted_iota(jnp.int32, (width, LANES), 0).astype(F32)

            def source(k, total):
                r_k = rsc[pl.ds(k, 1), :]
                c_k = csc[pl.ds(k, 1), :]
                w_k = wsc[pl.ds(k, 1), :]
                chosen = jnp.where(at == c_k, 1.0, 0.0).astype(BF16)
                for b in range(rows // block):
                    lines = dot(tab_ref[b * block * NF : (b + 1) * block * NF, :], chosen)
                    for j in range(block):
                        share = jnp.where(r_k == float(b * block + j), w_k, 0.0)
                        total = total + lines[j * NF : (j + 1) * NF] * share
                return total

            return lax.fori_loop(0, 4, source, jnp.zeros((NF, LANES), F32))

        drain(ps.at[0], crecv.at[0])
        ts[0 : WY * NF, 0:128] = both(ps)
        halo_send(ts, es, esl, esr, WY, WX, 0)

        send_lat(0)
        halo_recv(ts, es, esl, esr, WY, 0)
        send_lat(1)
        halo_sent(ts, es, esl, esr, WY, 0, 0, 2)
        ts[:, 128:256] = halo_columns(esl, esr, WY, 0).astype(BF16)

        for n, ref in ((12, aidx), (13, aw), (14, drv)):
            drain(ref, ld.at[n])

        def to_air(i, _):
            c = me * HC + i
            idx = jnp.concatenate(
                [aidx[t * NC + c] for t in range(LT)] + [jnp.zeros((4, LANES - LT * PM), jnp.int32)], axis=1
            )
            wgt = jnp.concatenate(
                [aw[t * NC + c] for t in range(LT)] + [jnp.ones((4, LANES - LT * PM), F32)], axis=1
            )
            ss[c] = regrid(ts, idx, wgt, OR, OC, 13 if OR % 13 == 0 else 1).astype(BF16)
            send(ss.at[c], sr.at[col], sss, ssr, (other, row, c))
            send(ss.at[c], ss.at[c], shs, shr, (other, row, col))

            @pl.when(c != col)
            def _():
                send(ss.at[c], sr.at[col], sss, ssr, (me, row, c))

            @pl.when(c == col)
            def _():
                pltpu.make_async_copy(ss.at[c], sr.at[col], ssr).start()

            return 0

        lax.fori_loop(0, HC, to_air, 0)
        send_lat(2)
        drain(tabt, ld.at[2])

        def analyse(t):
            drain(g1.at[t], g1r.at[t])

            def step(b, _):
                rows = pl.ds(pl.multiple_of(b * FB, FB), FB)
                ya[t, rows, :] = dot(tabt[rows, :], g1[t])
                return 0

            lax.fori_loop(0, 4, step, 0)

        analyse(0)
        lax.fori_loop(0, W8, pack_edges, 0)
        water_send(0, 8)
        send(water, x.at[me, 2 : 2 + WY, 0:WX], wsend.at[8, 0], wrecv.at[8, 0], (other, row, col))

        drv3[...] = jnp.zeros(drv3.shape, BF16)
        for t in range(LT):
            drv3[t, t * NF : (t + 1) * NF, :] = drv[...]
        drain(sr, ssr)
        for t in range(LT):
            st[t * NF : (t + 1) * NF, :] = jnp.concatenate(
                [sr[c].astype(F32)[:, t * PM : (t + 1) * PM] for c in range(NC)], axis=1
            ).astype(BF16)

        def analyse_fields(b, _):
            rows = pl.ds(pl.multiple_of(b * FB, FB), FB)
            us[rows, :] = dot_nt(tabt[rows, :], st[...]).astype(BF16)
            return 0

        lax.fori_loop(0, 4, analyse_fields, 0)
        pl.semaphore_wait(ready, NR - 1)

        HALVES = ((1, ND // 2), (ND // 2, ND))

        def scatter(t, h):
            if h == 0:
                pltpu.make_async_copy(sp.at[t, flat], rx.at[t, flat], r2.at[t]).start()

            def start(r_to, c_to):
                send(sp.at[t, r_to * NC + c_to], rx.at[t, flat], s2s.at[t, h], r2.at[t], (me, r_to, c_to))

            all_partners(h, start)

        def scattered(t, h):
            drain(sp.at[t, 0 : HALVES[h][1] - HALVES[h][0]], s2s.at[t, h])

        def force(t):
            def step(b, _):
                rows = pl.ds(pl.multiple_of(b * FB, FB), FB)
                got = ya[t, rows, :] + dot(us[rows, :], drv3[t])
                halves = [got[:, h * 128 : (h + 1) * 128].reshape(FB // 8, 8, 128) for h in range(2)]
                sp[t, pl.ds(b * (FB // 8), FB // 8)] = jnp.concatenate(halves, axis=1).astype(BF16)
                return 0

            lax.fori_loop(0, 4, step, 0)

        force(0)
        scatter(0, 0)
        scatter(0, 1)

        drain(atm_v, ld.at[0])
        drain(fwt, ld.at[11])

        def project_air(t, _):
            cells = atm_v[pl.ds(t * 4, 4)].reshape(4 * PM, C)
            got = dot_nt(fwt[...], cells)
            zeros = jnp.zeros((NF, 128 - PM), F32)
            for j in range(4):
                part = jnp.concatenate([got[:, j * PM : (j + 1) * PM], zeros], axis=1)
                pf[me, pl.ds((t * 4 + j) * NF, NF), :] = part.astype(BF16)
            return 0

        lax.fori_loop(0, PT // 4, project_air, 0)
        send(pf.at[me], pf.at[me], csend.at[1], crecv.at[1], (other, row, col))

        analyse(1)
        force(1)
        scattered(0, 0)
        scatter(1, 0)
        analyse(2)
        force(2)
        drain(pf.at[0], crecv.at[1])
        tf[0 : PT * NF, :] = both(pf)
        halo_send(tf, ef, efl, efr, PT, PM, 8)

        drain(ss.at[0:HC], shr)

        def lift_here(c, _):
            term = dot_tn(ss[c], drv[...])
            for t in range(LT):
                n = t * NC + c
                lf[n] = (atm_v[n].astype(F32) + term[t * PM : (t + 1) * PM]).astype(BF16)
            return 0

        lax.fori_loop(0, NC, lift_here, 0)

        scattered(0, 1)
        scatter(1, 1)

        drain(fb, ld.at[3])
        lat_in = lax.broadcasted_iota(jnp.int32, (NLAT, NLAT), 0)
        lat_to = lax.broadcasted_iota(jnp.int32, (NLAT, NLAT), 1)
        t_to, d_to = lat_to // ND, lax.rem(lat_to, ND)
        order = pick(lat_in == (d_to // NC) * PT + t_to * NC + lax.rem(d_to, NC))

        def reorder(k, _):
            fbp[k] = dot(fb[k], order).astype(BF16)
            return 0

        lax.fori_loop(0, KB, reorder, 0)

        halo_recv(tf, ef, efl, efr, PT, 8)
        halo_sent(tf, ef, efl, efr, PT, 8, 0, 2)
        tf[...] = (tf[...].astype(F32) + halo_columns(efl, efr, PT, PM)).astype(BF16)

        for n, ref in ((15, mask), (16, oidx), (17, ow), (18, flw)):
            drain(ref, ld.at[n])

        def to_ocean(j, _):
            i = me * HO + j
            idx = jnp.concatenate([oidx[2 * i], oidx[2 * i + 1]], axis=1)
            wgt = jnp.concatenate([ow[2 * i], ow[2 * i + 1]], axis=1)
            fx[i] = regrid(tf, idx, wgt, AR, AC, 10 if AR % 10 == 0 else 1).astype(BF16)
            send(fx.at[i], fx.at[i], fxs, fxr, (other, row, col))
            return 0

        lax.fori_loop(0, HO, to_ocean, 0)
        scattered(1, 0)
        scatter(2, 0)

        for q in range(2):
            for n, (there, dst) in enumerate(water_recvs(q)):
                @pl.when(there)
                def _(dst=dst, n=n, q=q):
                    drain(dst, wrecv.at[n, q])
        drain(x.at[0, 2 : 2 + WY, 0:WX], wrecv.at[8, 0])

        @pl.when(row == 0)
        def _():
            x[:, 0:2, 0:WX, :] = jnp.zeros((2, 2, WX, CO), BF16)

        @pl.when(row == NR - 1)
        def _():
            x[:, XR - 2 : XR, 0:WX, :] = jnp.zeros((2, 2, WX, CO), BF16)

        def side(i, tile, m, inside):
            for q in range(2):
                from_right = pltpu.roll(hr[q, tile].astype(F32), (16 - 2 * m) % 16, 0)
                from_left = pltpu.roll(hl[q, tile].astype(F32), (30 - 2 * m) % 16, 0)
                cells = jnp.where(
                    (sub < 2) & inside & (col < NC - 1),
                    from_right,
                    jnp.where((sub >= 14) & inside & (col > 0), from_left, 0.0),
                )
                x[q, i, WX:WP, :] = cells.astype(BF16)

        def sides(j, _):
            for m in range(8):
                side(2 + 8 * j + m, j, m, True)
            return 0

        lax.fori_loop(0, W8, sides, 0)
        for m in range(2):
            side(m, W8, 6 + m, row > 0)
            side(XR - 2 + m, W8 + 1, m, row < NR - 1)
        drain(w1, ld.at[8])

        def taps(src, weight, first, count):
            lhs = jnp.concatenate(
                [
                    jnp.concatenate([src[q, first + j + a] for a in range(3) for q in range(2)], axis=1)
                    for j in range(count)
                ],
                axis=0,
            )
            got = dot(lhs, weight[...])
            outs_ = []
            for j in range(count):
                part = got[j * WP : (j + 1) * WP]
                outs_.append(
                    pltpu.roll(part[:, 0:CO], 1, 0)
                    + part[:, CO : 2 * CO]
                    + pltpu.roll(part[:, 2 * CO : 3 * CO], WP - 1, 0)
                )
            return outs_

        def conv_first(i, _):
            place = lax.broadcasted_iota(jnp.int32, (WP, CO), 0)
            edge = ((place == WP - 1) & (col == 0)) | ((place == WX) & (col == NC - 1))
            for j, out in enumerate(taps(x, w1, 2 * i, 2)):
                h = 2 * i + j
                outside = ((h == 0) & (row == 0)) | ((h == HR_ - 1) & (row == NR - 1))
                hd[me, h] = jnp.where(edge | outside, 0.0, gelu(out)).astype(BF16)
            return 0

        lax.fori_loop(0, HR_ // 2, conv_first, 0)
        send(hd.at[me], hd.at[me], hds, hdr, (other, row, col))

        scattered(1, 1)
        scatter(2, 1)

        TB = 32 if ND % 32 == 0 else 8

        def widen(t):
            drain(rx.at[t], r2.at[t])

            def step(i, _):
                rows = pl.ds(pl.multiple_of(i * TB, TB), TB)
                out_rows = pl.ds(pl.multiple_of((t * ND + i * TB) * 16, TB * 16), TB * 16)
                rxf[out_rows, :] = rx[t, rows].astype(F32).reshape(TB * 16, 128)
                return 0

            lax.fori_loop(0, ND // TB, step, 0)

        def spectra_of(k, first, last):
            count = (last - first) * ND
            return jnp.concatenate(
                [rxf[pl.ds(first * ND * 16 + k + 8 * h, count, stride=16), :] for h in range(2)], axis=1
            ).astype(BF16)

        for t in range(LT - 1):
            widen(t)
        SPLIT = (LT - 1) * ND

        def to_modes_first(k, _):
            acc[k] = dot(fbp[k, :, 0:SPLIT], spectra_of(k, 0, LT - 1))
            return 0

        lax.fori_loop(0, KB, to_modes_first, 0)
        drain(mw, ld.at[5])
        drain(filt, ld.at[6])
        drain(ib, ld.at[4])
        widen(LT - 1)

        def to_modes(k, _):
            md[k] = (acc[k] + dot(fbp[k, :, SPLIT:NLAT], spectra_of(k, LT - 1, LT))).astype(BF16)
            send(md.at[k], mp.at[k], mds.at[k], mdr.at[k], (other, row, col))
            return 0

        lax.fori_loop(0, KB, to_modes, 0)

        def mix_own(k, _):
            acc[k] = dot(md[k], mw[pl.ds(pl.multiple_of(me * C, C), C), :])
            return 0

        lax.fori_loop(0, KB, mix_own, 0)

        def mix(k, _):
            drain(mp.at[k], mdr.at[k])
            mixed = acc[k] + dot(mp[k], mw[pl.ds(pl.multiple_of(other * C, C), C), :])
            ms[k] = (mixed * filt[...]).astype(BF16)
            return 0

        lax.fori_loop(0, KB, mix, 0)

        def gather_back(t, h):
            if h == 0:
                pltpu.make_async_copy(qb.at[t, flat], vx.at[t, flat], q_r.at[t]).start()

            def start(r_to, c_to):
                send(qb.at[t, r_to * NC + c_to], vx.at[t, flat], q_s.at[t, h], q_r.at[t], (me, r_to, c_to))

            all_partners(h, start)

        def gathered(t, h):
            drain(vx.at[t, 0 : HALVES[h][1] - HALVES[h][0]], q_s.at[t, h])

        def synth(t):
            def to_synth(k, _):
                basis = ib[k].reshape(NR, LT, NC, DEG)[:, t].reshape(ND, DEG)
                got = dot(basis, ms[k])
                for h in range(2):
                    qf[pl.ds(k + 8 * h, ND, stride=16), :] = got[:, h * 128 : (h + 1) * 128]
                return 0

            lax.fori_loop(0, KB, to_synth, 0)

            def narrow(i, _):
                rows = pl.ds(pl.multiple_of(i * TB, TB), TB)
                in_rows = pl.ds(pl.multiple_of(i * TB * 16, TB * 16), TB * 16)
                qb[t, rows] = qf[in_rows, :].reshape(TB, 16, 128).astype(BF16)
                return 0

            lax.fori_loop(0, ND // TB, narrow, 0)

        synth(0)
        gather_back(0, 0)
        gather_back(0, 1)
        synth(1)
        gathered(0, 0)
        gather_back(1, 0)
        synth(2)
        gathered(0, 1)
        gather_back(1, 1)

        drain(hd.at[0], hdr)
        drain(fx.at[0:HO], fxr)
        drain(w2, ld.at[9])

        def conv_second(i, _):
            outs_ = taps(hd, w2, 2 * i, 2)
            sixteenth = jnp.full((NF, CO), 1.0 / NF, BF16)
            for j in range(2):
                r = 2 * i + j
                lift = dot_tn(fx[i, :, j * WX : (j + 1) * WX], flw[...])
                line_mask = jnp.broadcast_to(mask[pl.ds(r, 1), :].astype(F32), (NF, WX)).astype(BF16)
                keep = dot_tn(line_mask, sixteenth)
                here = x[me, r + 2, 0:WX, :].astype(F32)
                oo[r] = (here + keep * (outs_[j][0:WX] + lift)).astype(BF16)
            return 0

        lax.fori_loop(0, WY // 2, conv_second, 0)
        pltpu.make_async_copy(oo, ocean_out, outs.at[0]).start()
        gathered(1, 0)
        gather_back(2, 0)

        drain(tab, ld.at[7])
        def to_grid(t):
            drain(vx.at[t], q_r.at[t])
            for h in range(2):
                part = vx[t].astype(F32)[:, 8 * h : 8 * h + 8, :].reshape(NLON, 128)
                bx[:, h * 128 : (h + 1) * 128] = part.astype(BF16)

            def synthesise(b, _):
                y = lax.rem(col // NX + b, NY)
                rows = pl.ds(pl.multiple_of(y * NX * PM, NX * PM), NX * PM)
                gs[t, rows, :] = dot(tab[rows, :], bx[...]).astype(BF16)

                def home(p, _):
                    there = y * NX + lax.rem(lax.rem(col, NX) + p, NX)

                    @pl.when(there != col)
                    def _():
                        send(gs.at[t, pl.ds(there * PM, PM)], hh.at[t * NC + col], gss.at[t], gsr.at[t],
                             (me, row, there))

                    @pl.when(there == col)
                    def _():
                        pltpu.make_async_copy(
                            gs.at[t, pl.ds(col * PM, PM)], hh.at[t * NC + col], gsr.at[t]
                        ).start()

                    return 0

                lax.fori_loop(0, NX, home, 0)
                return 0

            lax.fori_loop(0, NY, synthesise, 0)

        def finish_lats(t):
            drain(hh.at[t * NC : (t + 1) * NC], gsr.at[t])

            def finish(c, _):
                n = t * NC + c
                lf[n] = (lf[n].astype(F32) + gelu(hh[n].astype(F32))).astype(BF16)
                return 0

            lax.fori_loop(0, NC, finish, 0)
            done = pl.ds(t * NC, NC)
            pltpu.make_async_copy(lf.at[done], atm_out.at[done], outs.at[1]).start()

        to_grid(0)
        gathered(1, 1)
        gather_back(2, 1)
        to_grid(1)
        finish_lats(0)
        to_grid(2)
        finish_lats(1)
        finish_lats(2)

        for t in range(LT):
            drain(g1.at[t, 0 : (NC - 1) * PM], g1s.at[t])
            drain(gs.at[t, 0 : (NC - 1) * PM], gss.at[t])
        for h in range(2):
            scattered(LT - 1, h)
            gathered(LT - 1, h)
        drain(sr.at[0 : NC - 1], sss)

        @pl.when((col < me * HC) | (col >= me * HC + HC))
        def _():
            drain(sr.at[0], sss)

        drain(ss.at[0:HC], shs)
        drain(fx.at[0:HO], fxs)
        for q in range(2):
            for n, (there, src, dst, dev) in enumerate(water_sends(q)):
                @pl.when(there)
                def _(src=src, n=n, q=q):
                    drain(src, wsend.at[n, q])
        drain(water, wsend.at[8, 0])
        drain(ps.at[0], csend.at[0])
        drain(pf.at[0], csend.at[1])
        drain(hd.at[0], hds)
        for k in range(KB):
            drain(mp.at[k], mds.at[k])
        halo_sent(ts, es, esl, esr, WY, 0, 2, 8)
        halo_sent(tf, ef, efl, efr, PT, 8, 2, 8)
        drain(oo, outs.at[0])
        drain(lf, outs.at[1])

    v = pltpu.VMEM
    dma = pltpu.SemaphoreType.DMA
    scratch = [
        v((WY, WX), jnp.int32), v((WY, 4, WX), jnp.int32), v((WY, 4, WX), F32), v((PT, 4, PM), jnp.int32),
        v((PT, 4, PM), F32), v((NF, C), BF16), v((NF, CO), BF16), v((NF, CO), BF16), v((NF, C), BF16),
        v((LT, NLON, C), F32), v((NLON, LT * NF), BF16), v((LT * NF, NLON), BF16), v((LT, LT * NF, C), BF16),
        v((W8, 16, CO), BF16), v((W8, 16, CO), BF16),
        v((PT, PM, C), BF16), v((LT, NLON, C), BF16), v((NLON, NLON), BF16), v((NLON, NLON), BF16),
        v((LT, ND, 16, 128), BF16), v((LT, ND, 16, 128), BF16), v((NLAT * 16, 128), F32),
        v((KB, DEG, NLAT), BF16), v((KB, NLAT, DEG), BF16), v((KB, DEG, C), BF16), v((KB, DEG, C), BF16),
        v((2 * C, C), BF16), v((DEG, C), F32), v((ND * 16, 128), F32), v((LT, ND, 16, 128), BF16),
        v((LT, ND, 16, 128), BF16), v((NLON, C), BF16), v((LT, NLON, C), BF16), v((PT, PM, C), BF16), v((PT, PM, C), BF16),
        v((KB, DEG, NLAT), BF16), v((KB, DEG, C), F32), v((KB, DEG, C), BF16),
        v((2, XR, WP, CO), BF16), v((2, W8 + 2, 16, CO), BF16), v((2, W8 + 2, 16, CO), BF16), v((2, HR_, WP, CO), BF16),
        v((6 * CO, 3 * CO), BF16), v((6 * CO, 3 * CO), BF16), v((WY, WX, CO), BF16),
        v((AR * NF, 128), BF16), v((OR * NF, 256), BF16), v((2, PT * NF, 128), BF16), v((2, WY * NF, 128), BF16),
        v((16, PT * NF), BF16), v((16, WY * NF), BF16),
        v((3, 16, PT * NF), BF16), v((3, 16, PT * NF), BF16), v((3, 16, WY * NF), BF16), v((3, 16, WY * NF), BF16),
        v((4, LANES), F32), v((4, LANES), F32), v((4, LANES), F32),
        v((NC, NF, LANES), BF16), v((NC, NF, LANES), BF16), v((WY // 2, NF, LANES), BF16),
        dma((19,)), dma((9, 2)), dma((9, 2)), dma((2,)), dma((2,)), dma((16,)), dma((16,)),
        dma((LT,)), dma((LT,)), dma, dma, dma((LT, 2)), dma((LT,)), dma((KB,)), dma((KB,)),
        dma((LT, 2)), dma((LT,)), dma((LT,)), dma((LT,)), dma, dma, dma((2,)), dma, dma, dma, dma, pltpu.SemaphoreType.REGULAR,
    ]
    any_ = pl.BlockSpec(memory_space=pl.ANY)
    return pl.pallas_call(
        kernel,
        out_shape=(
            jax.ShapeDtypeStruct((PT, PM, C), BF16),
            jax.ShapeDtypeStruct((WY, WX, CO), BF16),
        ),
        in_specs=[any_] * 19,
        out_specs=(any_, any_),
        scratch_shapes=scratch,
        compiler_params=pltpu.CompilerParams(
            collective_id=0, has_side_effects=True, vmem_limit_bytes=60 * 1024 * 1024
        ),
        cost_estimate=pl.CostEstimate(flops=9_000_000_000, bytes_accessed=20_000_000, transcendentals=2_000_000),
        name="coupled_step",
    )


def solution(mesh):
    NR, NC = mesh.shape["row"], mesh.shape["col"]
    NX = 4 if NC == 16 else NC

    def local(
        atmosphere_state, water_condition, ocean_cell_mask, atmos_to_ocean_index, atmos_to_ocean_weight,
        water_source_positions, water_source_overlay_areas, flux_weight, flux_lift_weight,
        interface_projection_matrix, interface_driving_matrix, forward_basis, inverse_basis,
        mixing_weight, degree_filter, first_ocean_kernel, second_ocean_kernel,
    ):
        PT, PM, C = atmosphere_state.shape
        WY, WX, CO = water_condition.shape
        table = lon_table(NC * PM)
        step = make_kernel(
            NR, NC, NX, PT, PM, C, WY, WX, CO, flux_weight.shape[1], forward_basis.shape[1]
        )
        return step(
            atmosphere_state,
            water_condition,
            ocean_cell_mask,
            jnp.swapaxes(atmos_to_ocean_index, 1, 2),
            jnp.swapaxes(atmos_to_ocean_weight, 1, 2),
            jnp.swapaxes(water_source_positions, 1, 2),
            jnp.swapaxes(water_source_overlay_areas, 1, 2),
            flux_weight.T,
            flux_lift_weight,
            interface_projection_matrix.T,
            interface_driving_matrix,
            forward_basis,
            inverse_basis,
            mixing_weight,
            degree_filter,
            first_ocean_kernel,
            second_ocean_kernel,
            jnp.asarray(table),
            jnp.asarray(np.ascontiguousarray(table.T)),
        )

    placed = (
        P("row", "col", "comp"),
        P("row", "col", "comp"),
        P("row", "col"),
        P("row", "col", None),
        P("row", "col", None),
        P("row", "col", None),
        P("row", "col", None),
        P("comp", None),
        P(None, "comp"),
        P("comp", None),
        P(None, "comp"),
        P(("row", "col"), None, None),
        P(("row", "col"), None, None),
        P(None, "comp"),
        P(None, "comp"),
        P(None, None, None, "comp"),
        P(None, None, None, "comp"),
    )
    return jax.shard_map(
        local,
        mesh=mesh,
        in_specs=placed,
        out_specs=(P("row", "col", "comp"), P("row", "col", "comp")),
        check_vma=False,
    )
```
